256 devices in a mesh: ab: 16 (over z, y_lo), cd: 8 (over y_hi, x), rep: 2 (over core).
Axes of the slice: x: 4, y: 4 (y_hi: 2, y_lo: 2; y = y_hi * 2 + y_lo), z: 8, core: 2. Of those that a mesh axis runs over, the one named last changes fastest.
Arguments:
- integrals: bfloat16 [36864, 2048], P('ab', ('cd', 'rep')), may hold values from -0.125 to 0.125
- amplitudes: bfloat16 [13824, 2048], P(('cd', 'rep'), 'ab'), may hold values from -6 to 6
Outputs:
- ladder: bfloat16 [13824, 36864], P(('cd', 'rep'), 'ab')
The draws below stay inside these ranges and needn't reach their ends.
All inputs are finite; a program needn't handle non-finite values.
Results may differ from the reference program's by a relative error of at most 0.001.
Values may be sent and summed in bfloat16 or wider, within the bound.
A program may use at most 64 MiB of HBM per device.

```python
import jax
import jax.numpy as jnp
from jax import lax

NOCC = 48
NROOT = 6
PAIRS = 36864
QCOLS = 13824
KWIN = 2048


def block_scale(stream_key, shape, split, smallest, largest):
    gain = 1.0
    for position, shards_of in split:
        steps = jax.random.uniform(jax.random.fold_in(jax.random.fold_in(stream_key, 6), position), (shards_of,), jnp.float32, smallest / len(split), largest / len(split))
        gain = gain * jnp.repeat(jnp.exp(steps), shape[position] // shards_of).reshape((-1,) + (1,) * (len(shape) - 1 - position))
    return gain


def normal_values(rng, extent, spread, reach, shards=(), dtype=jnp.bfloat16):
    values = spread * jax.random.normal(rng, extent, jnp.float32)
    if shards:
        values = values * block_scale(rng, extent, shards, -0.22, 0.18)
    return jnp.clip(values, -reach, reach).astype(dtype)


def setup_inputs(seed: int = 0) -> dict:
    streams_of = jax.random.split(jax.random.key(seed), 3)
    integrals = normal_values(streams_of[0], (PAIRS, KWIN), KWIN ** -0.5, 0.125, ((0, 16), (1, 16)))
    amplitudes = normal_values(streams_of[1], (QCOLS, KWIN), 1.0, 6.0, ((0, 16), (1, 16)))
    return dict(integrals=integrals, amplitudes=amplitudes)


def reference(integrals, amplitudes):
    blocks = amplitudes.reshape(NROOT, NOCC * NOCC, KWIN)

    def one_root(rows_block):
        summed = jnp.dot(rows_block, integrals.T, preferred_element_type=jnp.float32)
        return summed.astype(jnp.bfloat16)

    return lax.map(one_root, blocks).reshape(QCOLS, PAIRS)
```

```python
import jax
import jax.numpy as jnp
from jax import lax
from jax.experimental import pallas as pl
from jax.experimental.pallas import tpu as pltpu
from jax.sharding import PartitionSpec as P

MESH = pl.DeviceIdType.MESH
ROWS = 864
COLS = 2304
BLK = 128
TILE = 256
NT = COLS // TILE
NA = 4
NB = NT - NA
ACH = 288
QP, QM, QY, QZ = 22, 23, 18, 21
AHEAD = 3
YLAG = 4
SLOTS = 24


def kernel(v_ref, r_ref, o_ref, vbuf, abuf, acc, lsem, xs, xr, ys, yr, ps, pr, zs, zr, cs, cr, os, orr):
    ab, cd, c = lax.axis_index("ab"), lax.axis_index("cd"), lax.axis_index("rep")
    z, yl = ab // 2, lax.rem(ab, 2)
    h, x = cd // 4, lax.rem(cd, 4)

    right, left = (ab, h * 4 + lax.rem(x + 1, 4), c), (ab, h * 4 + lax.rem(x + 3, 4), c)
    across = (ab, (1 - h) * 4 + x, c)
    pair = (z * 2 + 1 - yl, cd, c)
    up, down = (lax.rem(z + 1, 8) * 2 + yl, cd, c), (lax.rem(z + 7, 8) * 2 + yl, cd, c)
    sibling = (ab, cd, 1 - c)

    def remote(src, dst, s, r, to):
        return pltpu.make_async_remote_copy(
            src_ref=src, dst_ref=dst, send_sem=s, recv_sem=r, device_id=to, device_id_type=MESH
        )

    def where(conds, last):
        out = last
        for cond, value in reversed(conds):
            out = jnp.where(cond, value, out)
        return out

    def block(dx, dh):
        hh = h + dh - 2 * h * dh
        return hh * 4 + lax.rem(x + dx, 4)

    def tile_at(j, core, tile):
        return vbuf.at[2 * j + core, pl.ds(pl.multiple_of(tile * TILE, TILE), TILE)]

    def xp(q):
        dx = where([(q < 9, 0), (q < 13, 3), (q < 18, 0)], 3)
        dh = jnp.where(q < 13, 0, 1)
        return dx, dh, q - where([(q < 9, 0), (q < 18, 9)], 18)

    def xm(q):
        dx = where([(q < 9, 0), (q < 14, 1), (q < 18, 0)], 1)
        dh = jnp.where(q < 14, 0, 1)
        return dx, dh, where([(q < 5, q + 4), (q < 14, q - 5)], q - 14)

    def yx(p):
        first = p < 9
        i = jnp.where(first, p, p - 9)
        odd = lax.rem(i, 2)
        dx = jnp.where(first, 0, jnp.where(odd == 1, 3, 1))
        return dx, 0, jnp.where(odd == 1, i // 2, NA + i // 2)

    def xp_copy(q, shift=0, core=c):
        dx, dh, tile = xp(q)
        t = tile_at(block(dx + shift, dh), core, tile)
        return remote(t, t, xs.at[0, q], xr.at[0, q], right)

    def xm_copy(q, shift=0, core=c):
        dx, dh, tile = xm(q)
        t = tile_at(block(dx + shift, dh), core, tile)
        return remote(t, t, xs.at[1, q], xr.at[1, q], left)

    def y_copy(p, flip=0, core=c):
        dx, _, tile = yx(p)
        t = tile_at(block(dx, flip), core, tile)
        return remote(t, t, ys.at[p], yr.at[p], across)

    def a_at(zz, y, chunk):
        return abuf.at[2 * zz + y, pl.ds(pl.multiple_of(chunk * ACH, 16), ACH)]

    def zpart(r, way):
        k = r - 18
        lastp = jnp.where(k == 2, 1, 0) if way == 0 else jnp.where(k >= 1, 1, 0)
        lastc = jnp.where(k == 2, 0, k) if way == 0 else jnp.where(k == 0, 2, k)
        late = r >= 18
        part = jnp.where(late, lastp, lax.rem(r, 6) // 3)
        return r // 6 + 1, part, jnp.where(late, lastc, lax.rem(r, 3))

    def z_copy(s, way):
        k = s - 18
        if way == 0:
            tail = 12 + k + jnp.where(k == 2, 1, 0)
        else:
            tail = 14 + k + jnp.where(k >= 1, 1, 0)
        rr = jnp.where(s < 18, s, tail + 6)
        back, part, chunk = rr // 6, lax.rem(rr, 6) // 3, lax.rem(rr, 3)
        zz = lax.rem(z + (8 - back if way == 0 else back), 8)
        t = a_at(zz, jnp.where(part == 1, 1 - yl, yl), chunk)
        return remote(t, t, zs.at[way, s], zr.at[way, s], up if way == 0 else down)

    def z_arrival(r, way):
        back, part, chunk = zpart(r, way)
        zz = lax.rem(z + (8 - back if way == 0 else back), 8)
        t = a_at(zz, jnp.where(part == 1, 1 - yl, yl), chunk)
        return remote(t, t, zs.at[way, r], zr.at[way, r], up if way == 0 else down)

    def sib_copy(stream, q, core):
        if stream == 0:
            dx, dh, tile = xp(q)
            dx = dx + 3
        elif stream == 1:
            dx, dh, tile = xm(q)
            dx = dx + 1
        else:
            dx, _, tile = yx(q)
            dh = 1
        t = tile_at(block(dx, dh), core, tile)
        return remote(t, t, cs.at[stream, q], cr.at[stream, q], sibling)

    def pair_copy(i, y):
        t = a_at(z, y, i)
        return remote(t, t, ps.at[i], pr.at[i], pair)

    own_v = pltpu.make_async_copy(v_ref, vbuf.at[2 * cd + c], lsem.at[0])
    own_a = pltpu.make_async_copy(r_ref, abuf.at[2 * z + yl], lsem.at[1])
    own_a.start()
    own_v.start()

    barrier = pltpu.get_barrier_semaphore()
    for other in (right, left, across, pair, up, down, sibling):
        pl.semaphore_signal(barrier, inc=1, device_id=other, device_id_type=MESH)
    pl.semaphore_wait(barrier, 7)

    own_a.wait()
    for i in range(3):
        pair_copy(i, yl).start()
        z_copy(jnp.int32(i), 0).start()
        z_copy(jnp.int32(i), 1).start()
    own_v.wait()
    for i in range(AHEAD):
        xp_copy(jnp.int32(i)).start()
        xm_copy(jnp.int32(i)).start()
        if i < 2:
            y_copy(jnp.int32(i)).start()
    mine = vbuf.at[2 * cd + c]
    theirs = vbuf.at[2 * cd + 1 - c]
    remote(mine, mine, os.at[0], orr.at[0], sibling).start()
    acc[...] = jnp.zeros_like(acc)

    def product(j, tile, n):
        a = jnp.concatenate([abuf[2 * j], abuf[2 * j + 1]], axis=1)
        rows = pl.ds(pl.multiple_of(tile * TILE, TILE), n * TILE)
        b = jnp.concatenate([vbuf[2 * j, rows], vbuf[2 * j + 1, rows]], axis=1)
        return lax.dot_general(a, b, (((1,), (1,)), ((), ())), preferred_element_type=jnp.float32)

    def add(j, tile, n):
        part = product(j, tile, n)
        for k in range(n):
            acc[tile + k] += part[:, k * TILE : (k + 1) * TILE]

    def clip(v, top):
        return jnp.minimum(jnp.maximum(v, 0), top)

    def a_slot(j):
        d = lax.rem(j - z + 8, 8)
        d = jnp.minimum(d, 8 - d)
        return where([(d == 0, 3), (d == 1, 6), (d == 2, 13), (d == 3, 20)], SLOTS)

    def counts(j, t):
        jh, jx = j // 4, lax.rem(j, 4)
        dx = lax.rem(jx - x + 4, 4)
        nq, np_ = clip(t - 1, QM), clip(t - 5, QY)
        y1 = jnp.minimum(np_, 9)
        y2 = clip(np_ - 9, 9)
        same = jh == h
        first = where(
            [(same, where([(dx == 0, NA), (dx == 3, clip(nq, NA)), (dx == 1, clip(nq - 5, NA))], clip(nq - 9, NA))),
             (dx == 0, y1 // 2), (dx == 3, y2 // 2), (dx == 1, clip(nq - 14, NA))],
            clip(nq - 18, NA))
        second = where(
            [(same, where([(dx == 0, NB), (dx == 3, clip(nq - 4, NB)), (dx == 1, clip(nq, NB))], clip(nq - 9, NB))),
             (dx == 0, (y1 + 1) // 2), (dx == 3, clip(nq - 13, NB)), (dx == 1, (y2 + 1) // 2)],
            clip(nq - 18, NB))
        return first, second

    def zcount(t):
        return jnp.minimum(((t + 1) * 25) // 28, QZ)

    def xp_sent(t):
        return jnp.minimum(jnp.minimum(t + 1 + AHEAD, QP), 18 + jnp.maximum((t - 12) // 2, 0))

    def xm_sent(t):
        return jnp.minimum(jnp.minimum(t + 1 + AHEAD, QM), 18 + jnp.maximum((t - 11) // 2, 0))

    def slot(t, _):
        @pl.when(t < QP)
        def _():
            xp_copy(t, 3).wait_recv()
            sib_copy(0, t, c).start()

        @pl.when(t < QM)
        def _():
            xm_copy(t, 1).wait_recv()
            sib_copy(1, t, c).start()

        p = t - YLAG

        @pl.when(jnp.logical_and(p >= 0, p < QY))
        def _():
            y_copy(p, 1).wait_recv()
            sib_copy(2, p, c).start()

        def send(copy, lo, hi):
            def one(q, _):
                copy(q).start()
                return 0

            lax.fori_loop(lo, hi, one, 0)

        send(xp_copy, xp_sent(t - 1), xp_sent(t))
        send(xm_copy, xm_sent(t - 1), xm_sent(t))
        send(y_copy, jnp.minimum(t + 2, QY), jnp.minimum(t + 3, QY))

        def zstep(r, _):
            z_arrival(r, 0).wait_recv()
            z_arrival(r, 1).wait_recv()

            @pl.when(r < 3)
            def _():
                pair_copy(r, 1 - yl).wait_recv()

            @pl.when(r + 3 < QZ)
            def _():
                z_copy(r + 3, 0).start()
                z_copy(r + 3, 1).start()

            return 0

        lax.fori_loop(zcount(t - 1), zcount(t), zstep, 0)

        @pl.when(t == 0)
        def _():
            remote(theirs, theirs, os.at[0], orr.at[0], sibling).wait_recv()

        for stream, q, top in ((0, t - 1, QP), (1, t - 1, QM), (2, p - 1, QY)):

            @pl.when(jnp.logical_and(q >= 0, q < top))
            def _(stream=stream, q=q):
                sib_copy(stream, q, 1 - c).wait_recv()

        n_new = where([(t == 3, 1), (t == 6, 2), (t == 13, 2), (t == 20, 2)], 0)
        dist = where([(t == 3, 0), (t == 6, 1), (t == 13, 2)], 3)

        def catch_up(i, _):
            j = lax.rem(z + jnp.where(i == 0, dist, 8 - dist), 8)
            first, second = counts(j, t)

            def run(lo, n):
                def three(k, _):
                    add(j, lo + 3 * k, 3)
                    return 0

                lax.fori_loop(0, n // 3, three, 0)

                def one(k, _):
                    add(j, k, 1)
                    return 0

                lax.fori_loop(lo + 3 * (n // 3), lo + n, one, 0)

            whole = first == NA

            def part(k, _):
                lo = jnp.where(k == 0, 0, NA)
                run(lo, jnp.where(k == 0, jnp.where(whole, NA + second, first), second))
                return 0

            lax.fori_loop(0, jnp.where(whole, 1, 2), part, 0)
            return 0

        lax.fori_loop(0, n_new, catch_up, 0)

        def fresh(i, _):
            q = jnp.where(i == 2, p - 1, t - 1)
            dxp, dhp, tp = xp(q)
            dxm, dhm, tm = xm(q)
            dxy, _, ty = yx(q)
            dx = where([(i == 0, dxp + 3), (i == 1, dxm + 1)], dxy)
            dh = where([(i == 0, dhp), (i == 1, dhm)], 1)
            tile = where([(i == 0, tp), (i == 1, tm)], ty)
            top = where([(i == 0, QP), (i == 1, QM)], QY)
            j = block(dx, dh)

            @pl.when((q >= 0) & (q < top) & (a_slot(j) <= t))
            def _():
                add(j, tile, 1)

            return 0

        lax.fori_loop(0, 3, fresh, 0)
        return 0

    lax.fori_loop(0, SLOTS, slot, 0)

    j = lax.rem(z + 4, 8)

    def last(i, _):
        part = product(j, 3 * i, 3)
        for k in range(3):
            cols = pl.ds(pl.multiple_of((3 * i + k) * TILE, TILE), TILE)
            o_ref[:, cols] = (acc[3 * i + k] + part[:, k * TILE : (k + 1) * TILE]).astype(o_ref.dtype)
        return 0

    lax.fori_loop(0, NT // 3, last, 0)

    remote(mine, mine, os.at[0], orr.at[0], sibling).wait_send()

    def drain(top, *copies):
        def one(q, _):
            for copy in copies:
                copy(q).wait_send()
            return 0

        lax.fori_loop(0, top, one, 0)

    drain(QP, xp_copy, lambda q: sib_copy(0, q, c))
    drain(QM, xm_copy, lambda q: sib_copy(1, q, c))
    drain(QY, y_copy, lambda q: sib_copy(2, q, c))
    drain(QZ, lambda s: z_copy(s, 0), lambda s: z_copy(s, 1))
    drain(3, lambda i: pair_copy(i, yl))


def on_device(integrals, amplitudes):
    dma = pltpu.SemaphoreType.DMA
    return pl.pallas_call(
        kernel,
        out_shape=jax.ShapeDtypeStruct((ROWS, COLS), jnp.bfloat16),
        in_specs=[pl.BlockSpec(memory_space=pl.ANY)] * 2,
        out_specs=pl.BlockSpec(memory_space=pltpu.VMEM),
        scratch_shapes=[
            pltpu.VMEM((16, COLS, BLK), jnp.bfloat16),
            pltpu.VMEM((16, ROWS, BLK), jnp.bfloat16),
            pltpu.VMEM((NT, ROWS, TILE), jnp.float32),
            dma((2,)),
            dma((2, QM)), dma((2, QM)),
            dma((QY,)), dma((QY,)),
            dma((3,)), dma((3,)),
            dma((2, QZ)), dma((2, QZ)),
            dma((3, QM)), dma((3, QM)),
            dma((1,)), dma((1,)),
        ],
        compiler_params=pltpu.CompilerParams(
            collective_id=0, has_side_effects=True, vmem_limit_bytes=56 << 20
        ),
        cost_estimate=pl.CostEstimate(
            flops=2 * ROWS * COLS * 2048, bytes_accessed=5 << 20, transcendentals=0
        ),
        name="ladder",
    )(integrals, amplitudes)


def solution(mesh):
    in_specs = (P("ab", ("cd", "rep")), P(("cd", "rep"), "ab"))
    out_specs = P(("cd", "rep"), "ab")
    return jax.shard_map(on_device, mesh=mesh, in_specs=in_specs, out_specs=out_specs, check_vma=False)
```

```python
import jax
import jax.numpy as jnp
from jax import lax
from jax.experimental import pallas as pl
from jax.experimental.pallas import tpu as pltpu
from jax.sharding import PartitionSpec as P

MESH = pl.DeviceIdType.MESH
ROWS = 864
COLS = 2304
BLK = 128
TILE = 256
NT = COLS // TILE
ACH = 288
QX, QY, QZ = 23, 17, 21
AHEAD = 6
YAHEAD = 4
ZAHEAD = 3
XSEM, ZSEM, CSEM = 2 * AHEAD, 2 * ZAHEAD, 4
YLAG = 4
SLOTS = QX + 1


def z_count(t):
    return ((t + 1) * 25) // 28


OWN_SLOT, *A_SLOTS = [next(t for t in range(99) if z_count(t) >= n) for n in (3, 6, 12, 18)]
OWN_TILES = (3, 4, 5, 2, 1, 0, 6, 7, 8)
XP_HERE = [0] * 9 + [0, 1, 2, 3, 4] + [YLAG + p for p in (1, 2, 6, 7, 8, 9, 10, 13, 14)]
XM_HERE = [0] * 9 + [0, 1, 2, 3] + [YLAG + p for p in (1, 0, 3, 4, 5)] + [13] + [YLAG + p for p in (11, 12, 15, 16)]
XP_GROUPS = {2: 3, 5: 3, 8: 3, 11: 3, 13: 2, 16: 3, 18: 2, 21: 3, 22: 1}
XM_GROUPS = {1: 2, 4: 3, 7: 3, 8: 1, 10: 2, 12: 2, 14: 2, 17: 3, 18: 1, 20: 2, 22: 2}
Y_GROUPS = {2: 3, 5: 3, 8: 3, 10: 2, 12: 2, 14: 2, 16: 2}


def kernel(v_ref, r_ref, o_ref, vbuf, abuf, acc, lsem, xs, xr, ys, yr, ps, pr, zs, zr, cs, cr, orr):
    ab, cd, c = lax.axis_index("ab"), lax.axis_index("cd"), lax.axis_index("rep")
    z, yl = ab // 2, lax.rem(ab, 2)
    h, x = cd // 4, lax.rem(cd, 4)

    right, left = (ab, h * 4 + lax.rem(x + 1, 4), c), (ab, h * 4 + lax.rem(x + 3, 4), c)
    across = (ab, (1 - h) * 4 + x, c)
    pair = (z * 2 + 1 - yl, cd, c)
    up, down = (lax.rem(z + 1, 8) * 2 + yl, cd, c), (lax.rem(z + 7, 8) * 2 + yl, cd, c)
    sibling = (ab, cd, 1 - c)

    def remote(src, dst, s, r, to):
        return pltpu.make_async_remote_copy(
            src_ref=src, dst_ref=dst, send_sem=s, recv_sem=r, device_id=to, device_id_type=MESH
        )

    def where(conds, last):
        out = last
        for cond, value in reversed(conds):
            out = jnp.where(cond, value, out)
        return out

    def block(dx, dh):
        hh = h + dh - 2 * h * dh
        return hh * 4 + lax.rem(x + dx, 4)

    def tile_at(j, core, tile):
        return vbuf.at[2 * j + core, pl.ds(pl.multiple_of(tile * TILE, TILE), TILE)]

    def xp(q):
        dx = where([(q < 9, 0), (q < 14, 3), (q < 19, 0)], 3)
        dh = jnp.where(q < 14, 0, 1)
        return dx, dh, q - where([(q < 9, 0), (q < 14, 9), (q < 19, 10)], 19)

    def xm(q):
        dx = where([(q < 9, 0), (q < 13, 1), (q < 18, 0)], 1)
        dh = jnp.where(q < 13, 0, 1)
        return dx, dh, where([(q < 9, 8 - q), (q < 18, 17 - q), (q == 18, 4)], 27 - q)

    def yx(p):
        k = jnp.maximum(p - 9, 0)
        up_half = lax.rem(k // 2, 2) == 0
        i = (k // 4) * 2 + lax.rem(k, 2)
        dx = where([(p < 9, 0), (up_half, 3)], 1)
        return dx, 0, where([(p < 3, p + 3), (p < 6, 5 - p), (p < 9, p), (up_half, i)], 8 - i)

    def xp_copy(q, shift=0):
        dx, dh, tile = xp(q)
        t = tile_at(block(dx + shift, dh), c, tile)
        return remote(t, t, xs.at[0], xr.at[0, lax.rem(q, XSEM)], right)

    def xm_copy(q, shift=0):
        dx, dh, tile = xm(q)
        t = tile_at(block(dx + shift, dh), c, tile)
        return remote(t, t, xs.at[1], xr.at[1, lax.rem(q, XSEM)], left)

    def y_copy(p, flip=0):
        dx, _, tile = yx(p)
        t = tile_at(block(dx, flip), c, tile)
        return remote(t, t, ys.at[0], yr.at[p], across)

    def a_at(zz, y, chunk):
        return abuf.at[2 * zz + y, pl.ds(pl.multiple_of(chunk * ACH, 16), ACH)]

    def z_copy(s, way):
        k = s - 18
        if way == 0:
            tail = where([(k == 0, 12), (k == 1, 15)], 13)
        else:
            tail = where([(k == 0, 14), (k == 1, 17)], 16)
        rr = jnp.where(s < 18, s, tail + 6)
        back, part, chunk = rr // 6, lax.rem(rr, 6) // 3, lax.rem(rr, 3)
        zz = lax.rem(z + (8 - back if way == 0 else back), 8)
        t = a_at(zz, jnp.where(part == 1, 1 - yl, yl), chunk)
        return remote(t, t, zs.at[way], zr.at[way, lax.rem(s, ZSEM)], up if way == 0 else down)

    def z_arrival(r, way):
        k = r - 18
        if way == 0:
            part, chunk = jnp.where(k == 1, 1, 0), jnp.where(k == 2, 1, 0)
        else:
            part, chunk = jnp.where(k >= 1, 1, 0), jnp.where(k == 2, 1, 2)
        part = jnp.where(k >= 0, part, lax.rem(r, 6) // 3)
        chunk = jnp.where(k >= 0, chunk, lax.rem(r, 3))
        back = r // 6 + 1
        zz = lax.rem(z + (8 - back if way == 0 else back), 8)
        t = a_at(zz, jnp.where(part == 1, 1 - yl, yl), chunk)
        return remote(t, t, zs.at[way], zr.at[way, lax.rem(r, ZSEM)], up if way == 0 else down)

    def place(stream, q):
        if stream == 0:
            dx, dh, tile = xp(q)
            return block(dx + 3, dh), tile
        if stream == 1:
            dx, dh, tile = xm(q)
            return block(dx + 1, dh), tile
        dx, _, tile = yx(q)
        return block(dx, 1), tile

    def sib_copy(stream, q, core):
        j, tile = place(stream, q)
        t = tile_at(j, core, tile)
        return remote(t, t, cs.at[0], cr.at[stream, lax.rem(q, CSEM)], sibling)

    def pair_copy(i, y):
        t = a_at(z, y, i)
        return remote(t, t, ps.at[0], pr.at[i], pair)

    own_v = pltpu.make_async_copy(v_ref, vbuf.at[2 * cd + c], lsem.at[0])
    own_a = pltpu.make_async_copy(r_ref, abuf.at[2 * z + yl], lsem.at[1])
    own_a.start()
    own_v.start()

    barrier = pltpu.get_barrier_semaphore()
    for other in (right, left, across, pair, up, down, sibling):
        pl.semaphore_signal(barrier, inc=1, device_id=other, device_id_type=MESH)
    pl.semaphore_wait(barrier, 7)

    for i in range(3):
        rows = r_ref.at[pl.ds(i * ACH, ACH)]
        t = a_at(z, yl, i)
        remote(rows, t, ps.at[0], pr.at[i], pair).start()
        remote(rows, t, zs.at[0], zr.at[0, i], up).start()
        remote(rows, t, zs.at[1], zr.at[1, i], down).start()
    mine = vbuf.at[2 * cd + c]
    theirs = vbuf.at[2 * cd + 1 - c]
    for i in range(AHEAD):
        for tile, sem, to in ((i, 0, right), (8 - i, 1, left)):
            rows = v_ref.at[pl.ds(tile * TILE, TILE)]
            remote(rows, tile_at(cd, c, tile), xs.at[sem], xr.at[sem, i], to).start()
        if i < YAHEAD:
            tile = OWN_TILES[i]
            rows = v_ref.at[pl.ds(tile * TILE, TILE)]
            remote(rows, tile_at(cd, c, tile), ys.at[0], yr.at[i], across).start()
    remote(v_ref, mine, cs.at[0], orr.at[0], sibling).start()
    acc[...] = jnp.zeros_like(acc)
    own_a.wait()
    own_v.wait()

    def product(a, j, tile, n):
        rows = pl.ds(pl.multiple_of(tile * TILE, TILE), n * TILE)
        b = jnp.concatenate([vbuf[2 * j, rows], vbuf[2 * j + 1, rows]], axis=1)
        return lax.dot_general(a, b, (((1,), (1,)), ((), ())), preferred_element_type=jnp.float32)

    def add(j, tile, n):
        part = product(jnp.concatenate([abuf[2 * j], abuf[2 * j + 1]], axis=1), j, tile, n)
        for k in range(n):
            acc[tile + k] += part[:, k * TILE : (k + 1) * TILE]

    def clip(v, top):
        return jnp.minimum(jnp.maximum(v, 0), top)

    def a_slot(j):
        d = lax.rem(j - z + 8, 8)
        d = jnp.minimum(d, 8 - d)
        return where([(d == 0, OWN_SLOT), (d == 1, A_SLOTS[0]), (d == 2, A_SLOTS[1]), (d == 3, A_SLOTS[2])], SLOTS)

    def counts(j, t, run):
        jh, jx = j // 4, lax.rem(j, 4)
        dx = lax.rem(jx - x + 4, 4)
        nq, np_ = clip(t - 1, QX), clip(t - 1 - YLAG, QY)
        y1, y2 = jnp.minimum(np_, 9), clip(np_ - 9, 8)
        ya, yb = clip(y2, 2) + clip(y2 - 4, 2), clip(y2 - 2, 2) + clip(y2 - 6, 2)
        same = jh == h
        at0, at1, at3 = dx == 0, dx == 1, dx == 3

        def pick(near, far):
            return jnp.where(same, where([(at0, near[0]), (at1, near[1]), (at3, near[3])], near[2]),
                             where([(at0, far[0]), (at1, far[1]), (at3, far[3])], far[2]))

        n9 = clip(nq, 9)
        lo1 = pick((0, 9 - n9, 0, 0), (3 - clip(y1 - 3, 3), 5 - clip(nq - 13, 5), 0, 0))
        hi1 = pick((NT, NT, clip(nq - 9, 5), n9), (3 + clip(y1, 3), 5, clip(nq - 19, 4), ya))
        lo2 = pick((NT, NT, NT, NT), (6, NT, 4, 4))
        hi2 = pick((NT, NT, NT, NT), (6 + clip(y1 - 6, 3), NT, 4 + clip(nq - 18, 1), 4 + clip(nq - 14, 5)))
        n3 = pick((0, 0, clip(nq - 9, 4), 0), (0, yb, clip(nq - 19, 4), 0))
        lo = where([(run == 0, lo1), (run == 1, lo2)], NT - n3)
        return lo, where([(run == 0, hi1 - lo1), (run == 1, hi2 - lo2)], n3)

    def x_sent(t, here):
        out = jnp.minimum(t + 1 + AHEAD, QX)
        for q, slot in enumerate(here):
            if slot > q - AHEAD:
                out = jnp.minimum(out, jnp.where(t >= slot, QX, q)) if q >= AHEAD else out
        return out

    def y_sent(t):
        return jnp.minimum(t + 1 + YAHEAD, QY)

    def group(q, groups):
        return where([(q == last, n) for last, n in groups.items()], 0)

    def zstep(r, _):
        z_arrival(r, 0).wait_recv()
        z_arrival(r, 1).wait_recv()

        @pl.when(r < 3)
        def _():
            pair_copy(r, 1 - yl).wait_recv()

        @pl.when(r + ZAHEAD < QZ)
        def _():
            z_copy(r + ZAHEAD, 0).start()

        @pl.when((r + ZAHEAD < QZ) & (r != 16))
        def _():
            @pl.when(r == 17)
            def _():
                z_copy(r + ZAHEAD - 1, 1).start()

            z_copy(r + ZAHEAD, 1).start()

        return 0

    def send(copy, lo, hi):
        def one(q, _):
            copy(q).start()
            return 0

        lax.fori_loop(lo, hi, one, 0)

    def slot(t, _):
        p = t - YLAG

        @pl.when(t < QX)
        def _():
            xp_copy(t, 3).wait_recv()
            sib_copy(0, t, c).start()
            xm_copy(t, 1).wait_recv()
            sib_copy(1, t, c).start()

        @pl.when((p >= 0) & (p < QY))
        def _():
            y_copy(p, 1).wait_recv()
            sib_copy(2, p, c).start()

        send(xp_copy, x_sent(t - 1, XP_HERE), x_sent(t, XP_HERE))
        send(xm_copy, x_sent(t - 1, XM_HERE), x_sent(t, XM_HERE))
        send(y_copy, y_sent(t - 1), y_sent(t))
        lax.fori_loop(clip(z_count(t - 1), QZ - 1), clip(z_count(t), QZ - 1), zstep, 0)

        @pl.when(t == 0)
        def _():
            remote(theirs, theirs, cs.at[0], orr.at[0], sibling).wait_recv()

        @pl.when((t >= 1) & (t <= QX))
        def _():
            sib_copy(0, t - 1, 1 - c).wait_recv()
            sib_copy(1, t - 1, 1 - c).wait_recv()

        @pl.when((p >= 1) & (p <= QY))
        def _():
            sib_copy(2, p - 1, 1 - c).wait_recv()

        n_new = where([(t == OWN_SLOT, 1), (t == A_SLOTS[0], 2), (t == A_SLOTS[1], 2), (t == A_SLOTS[2], 2)], 0)
        dist = where([(t == OWN_SLOT, 0), (t == A_SLOTS[0], 1), (t == A_SLOTS[1], 2)], 3)

        def fresh(i):
            q = jnp.where(i == 2, p - 1, t - 1)
            j0, t0 = place(0, q)
            j1, t1 = place(1, q)
            j2, t2 = place(2, q)
            j = where([(i == 0, j0), (i == 1, j1)], j2)
            n = where([(i == 0, group(q, XP_GROUPS)), (i == 1, group(q, XM_GROUPS))], group(q, Y_GROUPS))
            n = jnp.minimum(clip(t - a_slot(j) + 1, 3), n)
            rising = (q < 3) | ((q >= 6) & (q < 11)) | (q == 13) | (q == 14)
            lo = where([(i == 0, t0 - n + 1), (i == 1, t1)], jnp.where(rising, t2 - n + 1, t2))
            return j, lo, n

        def caught_up(i):
            j = lax.rem(z + jnp.where(i < 6, dist, 8 - dist), 8)
            lo, n = counts(j, t, lax.rem(i, 3))
            return j, lo, n

        def work(i, _):
            j, lo, n = lax.cond(i < 3, fresh, caught_up, i)

            def three(k, _):
                add(j, lo + 3 * k, 3)
                return 0

            lax.fori_loop(0, n // 3, three, 0)
            more = lax.rem(n, 3)

            @pl.when(more == 2)
            def _():
                add(j, lo + n - 2, 2)

            @pl.when(more == 1)
            def _():
                add(j, lo + n - 1, 1)

            return 0

        lax.fori_loop(0, 3 + 3 * n_new, work, 0)
        return 0

    lax.fori_loop(0, SLOTS, slot, 0)

    j = lax.rem(z + 4, 8)

    def last(i, _):
        @pl.when(i == 2)
        def _():
            z_arrival(jnp.int32(QZ - 1), 0).wait_recv()
            z_arrival(jnp.int32(QZ - 1), 1).wait_recv()

        chunk = where([(i == 0, 0), (i == 1, 2)], 1)
        rows = pl.ds(pl.multiple_of(chunk * ACH, 16), ACH)
        a = jnp.concatenate([abuf[2 * j, rows], abuf[2 * j + 1, rows]], axis=1)
        for g in range(NT // 3):
            part = product(a, j, 3 * g, 3)
            for k in range(3):
                tile = 3 * g + k
                o_ref[rows, tile * TILE : (tile + 1) * TILE] = (
                    acc[tile, rows] + part[:, k * TILE : (k + 1) * TILE]
                ).astype(o_ref.dtype)
        return 0

    lax.fori_loop(0, 3, last, 0)

    def left_all(ref, sem, to):
        remote(ref, ref, sem, orr.at[0], to).wait_send()

    x_bytes = vbuf.at[pl.ds(0, 4), pl.ds(0, QX * TILE // 4)]
    left_all(x_bytes, xs.at[0], right)
    left_all(x_bytes, xs.at[1], left)
    left_all(vbuf.at[pl.ds(0, 2), pl.ds(0, QY * TILE // 2)], ys.at[0], across)
    left_all(abuf.at[pl.ds(0, QZ * ACH // ROWS)], zs.at[0], up)
    left_all(abuf.at[pl.ds(0, QZ * ACH // ROWS)], zs.at[1], down)
    left_all(abuf.at[0], ps.at[0], pair)
    left_all(vbuf.at[pl.ds(0, ((2 * QX + QY) * TILE + COLS) // COLS)], cs.at[0], sibling)


def on_device(integrals, amplitudes):
    dma = pltpu.SemaphoreType.DMA
    return pl.pallas_call(
        kernel,
        out_shape=pltpu.VMEM((ROWS, COLS), jnp.bfloat16),
        in_specs=[pl.BlockSpec(memory_space=pltpu.HBM)] * 2,
        out_specs=pl.BlockSpec(memory_space=pltpu.VMEM),
        scratch_shapes=[
            pltpu.VMEM((16, COLS, BLK), jnp.bfloat16),
            pltpu.VMEM((16, ROWS, BLK), jnp.bfloat16),
            pltpu.VMEM((NT, ROWS, TILE), jnp.float32),
            dma((2,)),
            dma((2,)), dma((2, XSEM)),
            dma((1,)), dma((QY,)),
            dma((1,)), dma((3,)),
            dma((2,)), dma((2, ZSEM)),
            dma((1,)), dma((3, CSEM)),
            dma((1,)),
        ],
        compiler_params=pltpu.CompilerParams(
            collective_id=0, has_side_effects=True, vmem_limit_bytes=59 << 20
        ),
        cost_estimate=pl.CostEstimate(
            flops=2 * ROWS * COLS * 2048, bytes_accessed=5 << 20, transcendentals=0
        ),
        name="ladder",
    )(integrals, amplitudes)


def solution(mesh):
    in_specs = (P("ab", ("cd", "rep")), P(("cd", "rep"), "ab"))
    out_specs = P(("cd", "rep"), "ab")
    return jax.shard_map(on_device, mesh=mesh, in_specs=in_specs, out_specs=out_specs, check_vma=False)
```

```python
import jax
import jax.numpy as jnp
from jax import lax
from jax.experimental import pallas as pl
from jax.experimental.pallas import tpu as pltpu
from jax.sharding import PartitionSpec as P

MESH = pl.DeviceIdType.MESH
ROWS = 864
COLS = 2304
BLK = 128
TILE = 256
NT = COLS // TILE
ACH = 288
QX, QY, QZ = 23, 17, 21
AHEAD = 6
YAHEAD = 4
ZAHEAD = 3
XSEM, ZSEM, CSEM = 2 * AHEAD, 2 * ZAHEAD, 4
YLAG = 4
SLOTS = QX + 1


def z_count(t):
    return ((t + 1) * 25) // 28


OWN_SLOT, *A_SLOTS = [next(t for t in range(99) if z_count(t) >= n) for n in (3, 6, 12, 18)]
OWN_TILES = (3, 4, 5, 2, 1, 0, 6, 7, 8)
XP_HERE = [0] * 9 + [0, 1, 2, 3, 4] + [YLAG + p for p in (1, 2, 6, 7, 8, 9, 10, 13, 14)]
XM_HERE = [0] * 9 + [0, 1, 2, 3] + [YLAG + p for p in (1, 0, 3, 4, 5)] + [13] + [YLAG + p for p in (11, 12, 15, 16)]

XP_GROUPS = {2: 3, 5: 3, 8: 3, 13: 5, 18: 5, 21: 3, 22: 1}
XM_GROUPS = {3: 4, 8: 5, 12: 4, 17: 5, 18: 1, 22: 4}
Y_GROUPS = {2: 3, 5: 3, 8: 3, 10: 2, 12: 2, 14: 2, 16: 2}


def kernel(v_ref, r_ref, o_ref, vbuf, abuf, acc, lsem, xs, xr, ys, yr, ps, pr, zs, zr, cs, cr, orr):
    ab, cd, c = lax.axis_index("ab"), lax.axis_index("cd"), lax.axis_index("rep")
    z, yl = ab // 2, lax.rem(ab, 2)
    h, x = cd // 4, lax.rem(cd, 4)

    right, left = (ab, h * 4 + lax.rem(x + 1, 4), c), (ab, h * 4 + lax.rem(x + 3, 4), c)
    across = (ab, (1 - h) * 4 + x, c)
    pair = (z * 2 + 1 - yl, cd, c)
    up, down = (lax.rem(z + 1, 8) * 2 + yl, cd, c), (lax.rem(z + 7, 8) * 2 + yl, cd, c)
    sibling = (ab, cd, 1 - c)

    def remote(src, dst, s, r, to):
        return pltpu.make_async_remote_copy(
            src_ref=src, dst_ref=dst, send_sem=s, recv_sem=r, device_id=to, device_id_type=MESH
        )

    def where(conds, last):
        out = last
        for cond, value in reversed(conds):
            out = jnp.where(cond, value, out)
        return out

    def block(dx, dh):
        hh = h + dh - 2 * h * dh
        return hh * 4 + lax.rem(x + dx, 4)

    def tile_at(j, core, tile):
        return vbuf.at[2 * j + core, pl.ds(pl.multiple_of(tile * TILE, TILE), TILE)]

    def xp(q):
        dx = where([(q < 9, 0), (q < 14, 3), (q < 19, 0)], 3)
        dh = jnp.where(q < 14, 0, 1)
        return dx, dh, q - where([(q < 9, 0), (q < 14, 9), (q < 19, 10)], 19)

    def xm(q):
        dx = where([(q < 9, 0), (q < 13, 1), (q < 18, 0)], 1)
        dh = jnp.where(q < 13, 0, 1)
        return dx, dh, where([(q < 9, 8 - q), (q < 18, 17 - q), (q == 18, 4)], 27 - q)

    def yx(p):
        k = jnp.maximum(p - 9, 0)
        up_half = lax.rem(k // 2, 2) == 0
        i = (k // 4) * 2 + lax.rem(k, 2)
        dx = where([(p < 9, 0), (up_half, 3)], 1)
        return dx, 0, where([(p < 3, p + 3), (p < 6, 5 - p), (p < 9, p), (up_half, i)], 8 - i)

    def xp_copy(q, shift=0):
        dx, dh, tile = xp(q)
        t = tile_at(block(dx + shift, dh), c, tile)
        return remote(t, t, xs.at[0], xr.at[0, lax.rem(q, XSEM)], right)

    def xm_copy(q, shift=0):
        dx, dh, tile = xm(q)
        t = tile_at(block(dx + shift, dh), c, tile)
        return remote(t, t, xs.at[1], xr.at[1, lax.rem(q, XSEM)], left)

    def y_copy(p, flip=0):
        dx, _, tile = yx(p)
        t = tile_at(block(dx, flip), c, tile)
        return remote(t, t, ys.at[0], yr.at[p], across)

    def a_at(zz, y, chunk):
        return abuf.at[2 * zz + y, pl.ds(pl.multiple_of(chunk * ACH, 16), ACH)]

    def z_copy(s, way):
        k = s - 18
        if way == 0:
            tail = where([(k == 0, 12), (k == 1, 15)], 13)
        else:
            tail = where([(k == 0, 14), (k == 1, 17)], 16)
        rr = jnp.where(s < 18, s, tail + 6)
        back, part, chunk = rr // 6, lax.rem(rr, 6) // 3, lax.rem(rr, 3)
        zz = lax.rem(z + (8 - back if way == 0 else back), 8)
        t = a_at(zz, jnp.where(part == 1, 1 - yl, yl), chunk)
        return remote(t, t, zs.at[way], zr.at[way, lax.rem(s, ZSEM)], up if way == 0 else down)

    def z_arrival(r, way):
        k = r - 18
        if way == 0:
            part, chunk = jnp.where(k == 1, 1, 0), jnp.where(k == 2, 1, 0)
        else:
            part, chunk = jnp.where(k >= 1, 1, 0), jnp.where(k == 2, 1, 2)
        part = jnp.where(k >= 0, part, lax.rem(r, 6) // 3)
        chunk = jnp.where(k >= 0, chunk, lax.rem(r, 3))
        back = r // 6 + 1
        zz = lax.rem(z + (8 - back if way == 0 else back), 8)
        t = a_at(zz, jnp.where(part == 1, 1 - yl, yl), chunk)
        return remote(t, t, zs.at[way], zr.at[way, lax.rem(r, ZSEM)], up if way == 0 else down)

    def place(stream, q):
        if stream == 0:
            dx, dh, tile = xp(q)
            return block(dx + 3, dh), tile
        if stream == 1:
            dx, dh, tile = xm(q)
            return block(dx + 1, dh), tile
        dx, _, tile = yx(q)
        return block(dx, 1), tile

    def sib_copy(stream, q, core):
        j, tile = place(stream, q)
        t = tile_at(j, core, tile)
        return remote(t, t, cs.at[0], cr.at[stream, lax.rem(q, CSEM)], sibling)

    def pair_copy(i, y):
        t = a_at(z, y, i)
        return remote(t, t, ps.at[0], pr.at[i], pair)

    own_v = pltpu.make_async_copy(v_ref, vbuf.at[2 * cd + c], lsem.at[0])
    own_a = pltpu.make_async_copy(r_ref, abuf.at[2 * z + yl], lsem.at[1])
    own_a.start()
    own_v.start()

    barrier = pltpu.get_barrier_semaphore()
    for other in (right, left, across, pair, up, down, sibling):
        pl.semaphore_signal(barrier, inc=1, device_id=other, device_id_type=MESH)
    pl.semaphore_wait(barrier, 7)

    for i in range(3):
        rows = r_ref.at[pl.ds(i * ACH, ACH)]
        t = a_at(z, yl, i)
        remote(rows, t, ps.at[0], pr.at[i], pair).start()
        remote(rows, t, zs.at[0], zr.at[0, i], up).start()
        remote(rows, t, zs.at[1], zr.at[1, i], down).start()
    mine = vbuf.at[2 * cd + c]
    theirs = vbuf.at[2 * cd + 1 - c]
    for i in range(AHEAD):
        for tile, sem, to in ((i, 0, right), (8 - i, 1, left)):
            rows = v_ref.at[pl.ds(tile * TILE, TILE)]
            remote(rows, tile_at(cd, c, tile), xs.at[sem], xr.at[sem, i], to).start()
        if i < YAHEAD:
            tile = OWN_TILES[i]
            rows = v_ref.at[pl.ds(tile * TILE, TILE)]
            remote(rows, tile_at(cd, c, tile), ys.at[0], yr.at[i], across).start()
    remote(v_ref, mine, cs.at[0], orr.at[0], sibling).start()
    acc[...] = jnp.zeros_like(acc)
    own_a.wait()
    own_v.wait()

    def product(a, j, tile, n):
        rows = pl.ds(pl.multiple_of(tile * TILE, TILE), n * TILE)
        b = jnp.concatenate([vbuf[2 * j, rows], vbuf[2 * j + 1, rows]], axis=1)
        return lax.dot_general(a, b, (((1,), (1,)), ((), ())), preferred_element_type=jnp.float32)

    def add(j, tile, n):
        part = product(jnp.concatenate([abuf[2 * j], abuf[2 * j + 1]], axis=1), j, tile, n)
        for k in range(n):
            acc[tile + k] += part[:, k * TILE : (k + 1) * TILE]

    def clip(v, top):
        return jnp.minimum(jnp.maximum(v, 0), top)

    def a_slot(j):
        d = lax.rem(j - z + 8, 8)
        d = jnp.minimum(d, 8 - d)
        return where([(d == 0, OWN_SLOT), (d == 1, A_SLOTS[0]), (d == 2, A_SLOTS[1]), (d == 3, A_SLOTS[2])], SLOTS)

    def came(j, tile):
        jh, jx = j // 4, lax.rem(j, 4)
        dx = lax.rem(jx - x + 4, 4)
        low = tile < 4
        pos = where([(tile < 3, 5 - tile), (tile < 6, tile - 3)], tile)
        rise = where([(tile < 2, 9 + tile)], 11 + tile) + YLAG + 1
        fall = where([(tile > 6, 19 - tile)], 21 - tile) + YLAG + 1
        near = where([(dx == 0, 0), (dx == 1, 9 - tile), (dx == 3, tile + 1), (tile < 5, tile + 10)], 18 - tile)
        far = where(
            [(dx == 0, pos + YLAG + 1), (dx == 1, jnp.where(tile < 5, 18 - tile, fall)),
             (dx == 3, jnp.where(low, rise, tile + 11)), (low, tile + 20), (tile == 4, 19)],
            28 - tile)
        return jnp.where(jh == h, near, far)

    def all_came(j):
        dx = lax.rem(lax.rem(j, 4) - x + 4, 4)
        near = where([(dx == 0, 0), (dx == 2, 14)], 9)
        far = where([(dx == 0, YLAG + 9), (dx == 3, 19), (dx == 1, YLAG + 17)], QX)
        return jnp.where(j // 4 == h, near, far)

    def x_sent(t, here):
        out = jnp.minimum(t + 1 + AHEAD, QX)
        for q, slot in enumerate(here):
            if slot > q - AHEAD:
                out = jnp.minimum(out, jnp.where(t >= slot, QX, q)) if q >= AHEAD else out
        return out

    def y_sent(t):
        return jnp.minimum(t + 1 + YAHEAD, QY)

    def group(q, groups):
        return where([(q == last, n) for last, n in groups.items()], 0)

    def zstep(r, _):
        z_arrival(r, 0).wait_recv()
        z_arrival(r, 1).wait_recv()

        @pl.when(r < 3)
        def _():
            pair_copy(r, 1 - yl).wait_recv()

        @pl.when(r + ZAHEAD < QZ)
        def _():
            z_copy(r + ZAHEAD, 0).start()

        @pl.when((r + ZAHEAD < QZ) & (r != 16))
        def _():
            @pl.when(r == 17)
            def _():
                z_copy(r + ZAHEAD - 1, 1).start()

            z_copy(r + ZAHEAD, 1).start()

        return 0

    def send(copy, lo, hi):
        def one(q, _):
            copy(q).start()
            return 0

        lax.fori_loop(lo, hi, one, 0)

    def slot(t, _):
        p = t - YLAG

        @pl.when(t < QX)
        def _():
            xp_copy(t, 3).wait_recv()
            sib_copy(0, t, c).start()
            xm_copy(t, 1).wait_recv()
            sib_copy(1, t, c).start()

        @pl.when((p >= 0) & (p < QY))
        def _():
            y_copy(p, 1).wait_recv()
            sib_copy(2, p, c).start()

        send(xp_copy, x_sent(t - 1, XP_HERE), x_sent(t, XP_HERE))
        send(xm_copy, x_sent(t - 1, XM_HERE), x_sent(t, XM_HERE))
        send(y_copy, y_sent(t - 1), y_sent(t))
        lax.fori_loop(clip(z_count(t - 1), QZ - 1), clip(z_count(t), QZ - 1), zstep, 0)

        @pl.when(t == 0)
        def _():
            remote(theirs, theirs, cs.at[0], orr.at[0], sibling).wait_recv()

        @pl.when((t >= 1) & (t <= QX))
        def _():
            sib_copy(0, t - 1, 1 - c).wait_recv()
            sib_copy(1, t - 1, 1 - c).wait_recv()

        @pl.when((p >= 1) & (p <= QY))
        def _():
            sib_copy(2, p - 1, 1 - c).wait_recv()

        def fresh(i):
            q = jnp.where(i == 2, p - 1, t - 1)
            full = where([(i == 0, group(q, XP_GROUPS)), (i == 1, group(q, XM_GROUPS))], group(q, Y_GROUPS))

            def due():
                j0, t0 = place(0, q)
                j1, t1 = place(1, q)
                j2, t2 = place(2, q)
                j = where([(i == 0, j0), (i == 1, j1)], j2)
                n = jnp.minimum(clip(t - a_slot(j) + 1, 5), full)
                rising = (q < 3) | ((q >= 6) & (q < 11)) | (q == 13) | (q == 14)
                lo = where([(i == 0, t0 - n + 1), (i == 1, t1)], jnp.where(rising, t2 - n + 1, t2))
                return j, lo, n, jnp.int32(0)

            return lax.cond(full > 0, due, lambda: (jnp.int32(0),) * 4)

        event = where([(t < A_SLOTS[0], OWN_SLOT), (t < A_SLOTS[1], A_SLOTS[0]), (t < A_SLOTS[2], A_SLOTS[1])], A_SLOTS[2])
        dist = where([(t < A_SLOTS[0], 0), (t < A_SLOTS[1], 1), (t < A_SLOTS[2], 2)], 3)
        busy = (t == event) | ((t == event + 1) & (dist > 0))

        def waited(i):
            j = lax.rem(z + jnp.where(t == event, dist, 8 - dist), 8)
            whole = all_came(j) < event

            def part():
                lo = 3 * (i - 3)
                b0, b1, b2 = [jnp.where(came(j, lo + m) < event, 1, 0) for m in range(3)]
                n = b0 + b1 + b2
                gap = jnp.where((n == 2) & (b1 == 0), 1, 0)
                return j, lo + jnp.where(b0 == 1, 0, jnp.where(b1 == 1, 1, 2)), n, gap

            return lax.cond(whole, lambda: (j, jnp.int32(0), jnp.where(i == 3, NT, 0), jnp.int32(0)), part)

        def work(i, _):
            j, lo, n, gap = lax.cond(i < 3, fresh, waited, i)
            for size in (2, 3, 4, 5, NT):

                @pl.when((n == size) & (gap == 0))
                def _(size=size):
                    add(j, lo if size < NT else 0, size)

            def one(m, _):
                add(j, lo + 2 * m, 1)
                return 0

            lax.fori_loop(0, where([(n == 1, 1), (gap == 1, 2)], 0), one, 0)
            return 0

        lax.fori_loop(0, jnp.where(busy, 6, 3), work, 0)
        return 0

    lax.fori_loop(0, SLOTS, slot, 0)

    j = lax.rem(z + 4, 8)

    z_arrival(jnp.int32(QZ - 1), 0).wait_recv()
    z_arrival(jnp.int32(QZ - 1), 1).wait_recv()
    part = product(jnp.concatenate([abuf[2 * j], abuf[2 * j + 1]], axis=1), j, 0, NT)
    for k in range(NT):
        cols = slice(k * TILE, (k + 1) * TILE)
        o_ref[:, cols] = (acc[k] + part[:, cols]).astype(o_ref.dtype)

    def left_all(ref, sem, to):
        remote(ref, ref, sem, orr.at[0], to).wait_send()

    x_bytes = vbuf.at[pl.ds(0, 4), pl.ds(0, QX * TILE // 4)]
    left_all(x_bytes, xs.at[0], right)
    left_all(x_bytes, xs.at[1], left)
    left_all(vbuf.at[pl.ds(0, 2), pl.ds(0, QY * TILE // 2)], ys.at[0], across)
    left_all(abuf.at[pl.ds(0, QZ * ACH // ROWS)], zs.at[0], up)
    left_all(abuf.at[pl.ds(0, QZ * ACH // ROWS)], zs.at[1], down)
    left_all(abuf.at[0], ps.at[0], pair)
    left_all(vbuf.at[pl.ds(0, ((2 * QX + QY) * TILE + COLS) // COLS)], cs.at[0], sibling)


def on_device(integrals, amplitudes):
    dma = pltpu.SemaphoreType.DMA
    return pl.pallas_call(
        kernel,
        out_shape=pltpu.VMEM((ROWS, COLS), jnp.bfloat16),
        in_specs=[pl.BlockSpec(memory_space=pltpu.HBM)] * 2,
        out_specs=pl.BlockSpec(memory_space=pltpu.VMEM),
        scratch_shapes=[
            pltpu.VMEM((16, COLS, BLK), jnp.bfloat16),
            pltpu.VMEM((16, ROWS, BLK), jnp.bfloat16),
            pltpu.VMEM((NT, ROWS, TILE), jnp.float32),
            dma((2,)),
            dma((2,)), dma((2, XSEM)),
            dma((1,)), dma((QY,)),
            dma((1,)), dma((3,)),
            dma((2,)), dma((2, ZSEM)),
            dma((1,)), dma((3, CSEM)),
            dma((1,)),
        ],
        compiler_params=pltpu.CompilerParams(
            collective_id=0, has_side_effects=True, vmem_limit_bytes=59 << 20
        ),
        cost_estimate=pl.CostEstimate(
            flops=2 * ROWS * COLS * 2048, bytes_accessed=5 << 20, transcendentals=0
        ),
        name="ladder",
    )(integrals, amplitudes)


def solution(mesh):
    in_specs = (P("ab", ("cd", "rep")), P(("cd", "rep"), "ab"))
    out_specs = P(("cd", "rep"), "ab")
    return jax.shard_map(on_device, mesh=mesh, in_specs=in_specs, out_specs=out_specs, check_vma=False)
```

```python
import jax
import jax.numpy as jnp
from jax import lax
from jax.experimental import pallas as pl
from jax.experimental.pallas import tpu as pltpu
from jax.sharding import PartitionSpec as P

MESH = pl.DeviceIdType.MESH
ROWS = 864
COLS = 2304
BLK = 128
TILE = 256
NT = COLS // TILE
ACH = 288
QX, QY, QZ = 23, 17, 21
AHEAD = 6
YAHEAD = 4
ZAHEAD = 3
XSEM, ZSEM, CSEM = 2 * AHEAD, 2 * ZAHEAD, 4
YLAG = 4
SLOTS = QX + 1
CUTS = ((0, 3), (3, 6), (6, 9))


def z_count(t):
    return ((t + 1) * 25) // 28


OWN_SLOT, *A_SLOTS = [next(t for t in range(99) if z_count(t) >= n) for n in (3, 6, 12, 18)]
OWN_TILES = (3, 4, 5, 2, 1, 0, 6, 7, 8)
XP_HERE = [0] * 9 + [0, 1, 2, 3, 4] + [YLAG + p for p in (1, 2, 6, 7, 8, 9, 10, 13, 14)]
XM_HERE = [0] * 9 + [0, 1, 2, 3] + [YLAG + p for p in (1, 0, 3, 4, 5)] + [13] + [YLAG + p for p in (11, 12, 15, 16)]

XP_GROUPS = {2: 3, 5: 3, 8: 3, 13: 5, 18: 5}
XM_GROUPS = {3: 4, 8: 5, 12: 4, 17: 5}
Y_GROUPS = {2: 3, 5: 3, 8: 3, 10: 2, 12: 2, 14: 2, 16: 2}


def kernel(v_ref, r_ref, vbuf, abuf, acc, lsem, xs, xr, ys, yr, ps, pr, zs, zr, cs, cr, orr):
    ab, cd, c = lax.axis_index("ab"), lax.axis_index("cd"), lax.axis_index("rep")
    z, yl = ab // 2, lax.rem(ab, 2)
    h, x = cd // 4, lax.rem(cd, 4)

    right, left = (ab, h * 4 + lax.rem(x + 1, 4), c), (ab, h * 4 + lax.rem(x + 3, 4), c)
    across = (ab, (1 - h) * 4 + x, c)
    pair = (z * 2 + 1 - yl, cd, c)
    up, down = (lax.rem(z + 1, 8) * 2 + yl, cd, c), (lax.rem(z + 7, 8) * 2 + yl, cd, c)
    sibling = (ab, cd, 1 - c)

    def remote(src, dst, s, r, to):
        return pltpu.make_async_remote_copy(
            src_ref=src, dst_ref=dst, send_sem=s, recv_sem=r, device_id=to, device_id_type=MESH
        )

    def where(conds, last):
        out = last
        for cond, value in reversed(conds):
            out = jnp.where(cond, value, out)
        return out

    def block(dx, dh):
        hh = h + dh - 2 * h * dh
        return hh * 4 + lax.rem(x + dx, 4)

    def tile_at(j, core, tile):
        return vbuf.at[2 * j + core, pl.ds(pl.multiple_of(tile * TILE, TILE), TILE)]

    def xp(q):
        dx = where([(q < 9, 0), (q < 14, 3), (q < 19, 0)], 3)
        dh = jnp.where(q < 14, 0, 1)
        return dx, dh, q - where([(q < 9, 0), (q < 14, 9), (q < 19, 10)], 19)

    def xm(q):
        dx = where([(q < 9, 0), (q < 13, 1), (q < 18, 0)], 1)
        dh = jnp.where(q < 13, 0, 1)
        return dx, dh, where([(q < 9, 8 - q), (q < 18, 17 - q), (q == 18, 4)], 27 - q)

    def yx(p):
        k = jnp.maximum(p - 9, 0)
        up_half = lax.rem(k // 2, 2) == 0
        i = (k // 4) * 2 + lax.rem(k, 2)
        dx = where([(p < 9, 0), (up_half, 3)], 1)
        return dx, 0, where([(p < 3, p + 3), (p < 6, 5 - p), (p < 9, p), (up_half, i)], 8 - i)

    def xp_copy(q, shift=0):
        dx, dh, tile = xp(q)
        t = tile_at(block(dx + shift, dh), c, tile)
        return remote(t, t, xs.at[0], xr.at[0, lax.rem(q, XSEM)], right)

    def xm_copy(q, shift=0):
        dx, dh, tile = xm(q)
        t = tile_at(block(dx + shift, dh), c, tile)
        return remote(t, t, xs.at[1], xr.at[1, lax.rem(q, XSEM)], left)

    def y_copy(p, flip=0):
        dx, _, tile = yx(p)
        t = tile_at(block(dx, flip), c, tile)
        return remote(t, t, ys.at[0], yr.at[p], across)

    def a_at(zz, y, chunk):
        return abuf.at[2 * zz + y, pl.ds(pl.multiple_of(chunk * ACH, 16), ACH)]

    def z_copy(s, way):
        k = s - 18
        if way == 0:
            tail = where([(k == 0, 12), (k == 1, 15)], 13)
        else:
            tail = where([(k == 0, 14), (k == 1, 17)], 16)
        rr = jnp.where(s < 18, s, tail + 6)
        back, part, chunk = rr // 6, lax.rem(rr, 6) // 3, lax.rem(rr, 3)
        zz = lax.rem(z + (8 - back if way == 0 else back), 8)
        t = a_at(zz, jnp.where(part == 1, 1 - yl, yl), chunk)
        return remote(t, t, zs.at[way], zr.at[way, lax.rem(s, ZSEM)], up if way == 0 else down)

    def z_arrival(r, way):
        k = r - 18
        if way == 0:
            part, chunk = jnp.where(k == 1, 1, 0), jnp.where(k == 2, 1, 0)
        else:
            part, chunk = jnp.where(k >= 1, 1, 0), jnp.where(k == 2, 1, 2)
        part = jnp.where(k >= 0, part, lax.rem(r, 6) // 3)
        chunk = jnp.where(k >= 0, chunk, lax.rem(r, 3))
        back = r // 6 + 1
        zz = lax.rem(z + (8 - back if way == 0 else back), 8)
        t = a_at(zz, jnp.where(part == 1, 1 - yl, yl), chunk)
        return remote(t, t, zs.at[way], zr.at[way, lax.rem(r, ZSEM)], up if way == 0 else down)

    def place(stream, q):
        if stream == 0:
            dx, dh, tile = xp(q)
            return block(dx + 3, dh), tile
        if stream == 1:
            dx, dh, tile = xm(q)
            return block(dx + 1, dh), tile
        dx, _, tile = yx(q)
        return block(dx, 1), tile

    def sib_copy(stream, q, core):
        j, tile = place(stream, q)
        t = tile_at(j, core, tile)
        return remote(t, t, cs.at[0], cr.at[stream, lax.rem(q, CSEM)], sibling)

    def pair_copy(i, y):
        t = a_at(z, y, i)
        return remote(t, t, ps.at[0], pr.at[i], pair)

    own_v = pltpu.make_async_copy(v_ref, vbuf.at[2 * cd + c], lsem.at[0])
    own_a = pltpu.make_async_copy(r_ref, abuf.at[2 * z + yl], lsem.at[1])
    own_a.start()
    own_v.start()

    barrier = pltpu.get_barrier_semaphore()
    for other in (right, left, across, pair, up, down, sibling):
        pl.semaphore_signal(barrier, inc=1, device_id=other, device_id_type=MESH)
    pl.semaphore_wait(barrier, 7)

    for i in range(3):
        rows = r_ref.at[pl.ds(i * ACH, ACH)]
        t = a_at(z, yl, i)
        remote(rows, t, ps.at[0], pr.at[i], pair).start()
        remote(rows, t, zs.at[0], zr.at[0, i], up).start()
        remote(rows, t, zs.at[1], zr.at[1, i], down).start()
    mine = vbuf.at[2 * cd + c]
    theirs = vbuf.at[2 * cd + 1 - c]
    for i in range(AHEAD):
        for tile, sem, to in ((i, 0, right), (8 - i, 1, left)):
            rows = v_ref.at[pl.ds(tile * TILE, TILE)]
            remote(rows, tile_at(cd, c, tile), xs.at[sem], xr.at[sem, i], to).start()
        if i < YAHEAD:
            tile = OWN_TILES[i]
            rows = v_ref.at[pl.ds(tile * TILE, TILE)]
            remote(rows, tile_at(cd, c, tile), ys.at[0], yr.at[i], across).start()
    remote(v_ref, mine, cs.at[0], orr.at[0], sibling).start()
    acc[...] = jnp.zeros_like(acc)
    own_a.wait()
    own_v.wait()

    def product(a, j, tile, n):
        rows = pl.ds(pl.multiple_of(tile * TILE, TILE), n * TILE)
        b = jnp.concatenate([vbuf[2 * j, rows], vbuf[2 * j + 1, rows]], axis=1)
        return lax.dot_general(a, b, (((1,), (1,)), ((), ())), preferred_element_type=jnp.float32)

    def add(j, tile, n):
        part = product(jnp.concatenate([abuf[2 * j], abuf[2 * j + 1]], axis=1), j, tile, n)
        for k in range(n):
            acc[tile + k] += part[:, k * TILE : (k + 1) * TILE]

    def clip(v, top):
        return jnp.minimum(jnp.maximum(v, 0), top)

    def a_slot(j):
        d = lax.rem(j - z + 8, 8)
        d = jnp.minimum(d, 8 - d)
        return where([(d == 0, OWN_SLOT), (d == 1, A_SLOTS[0]), (d == 2, A_SLOTS[1]), (d == 3, A_SLOTS[2])], SLOTS)

    def came(j, tile):
        jh, jx = j // 4, lax.rem(j, 4)
        dx = lax.rem(jx - x + 4, 4)
        low = tile < 4
        pos = where([(tile < 3, 5 - tile), (tile < 6, tile - 3)], tile)
        rise = where([(tile < 2, 9 + tile)], 11 + tile) + YLAG + 1
        fall = where([(tile > 6, 19 - tile)], 21 - tile) + YLAG + 1
        near = where([(dx == 0, 0), (dx == 1, 9 - tile), (dx == 3, tile + 1), (tile < 5, tile + 10)], 18 - tile)
        far = where(
            [(dx == 0, pos + YLAG + 1), (dx == 1, jnp.where(tile < 5, 18 - tile, fall)),
             (dx == 3, jnp.where(low, rise, tile + 11))],
            99)
        return jnp.where(jh == h, near, far)

    def all_came(j):
        dx = lax.rem(lax.rem(j, 4) - x + 4, 4)
        near = where([(dx == 0, 0), (dx == 2, 14)], 9)
        far = where([(dx == 0, YLAG + 9), (dx == 3, 19), (dx == 1, YLAG + 17)], QX)
        return jnp.where(j // 4 == h, near, far)

    def x_sent(t, here):
        out = jnp.minimum(t + 1 + AHEAD, QX)
        for q, slot in enumerate(here):
            if slot > q - AHEAD:
                out = jnp.minimum(out, jnp.where(t >= slot, QX, q)) if q >= AHEAD else out
        return out

    def y_sent(t):
        return jnp.minimum(t + 1 + YAHEAD, QY)

    def group(q, groups):
        return where([(q == last, n) for last, n in groups.items()], 0)

    def zstep(r, _):
        z_arrival(r, 0).wait_recv()
        z_arrival(r, 1).wait_recv()

        @pl.when(r < 3)
        def _():
            pair_copy(r, 1 - yl).wait_recv()

        @pl.when(r + ZAHEAD < QZ)
        def _():
            z_copy(r + ZAHEAD, 0).start()

        @pl.when((r + ZAHEAD < QZ) & (r != 16))
        def _():
            @pl.when(r == 17)
            def _():
                z_copy(r + ZAHEAD - 1, 1).start()

            z_copy(r + ZAHEAD, 1).start()

        return 0

    def send(copy, lo, hi):
        def one(q, _):
            copy(q).start()
            return 0

        lax.fori_loop(lo, hi, one, 0)

    def slot(t, _):
        p = t - YLAG

        @pl.when(t < QX)
        def _():
            xp_copy(t, 3).wait_recv()
            sib_copy(0, t, c).start()
            xm_copy(t, 1).wait_recv()
            sib_copy(1, t, c).start()

        @pl.when((p >= 0) & (p < QY))
        def _():
            y_copy(p, 1).wait_recv()
            sib_copy(2, p, c).start()

        send(xp_copy, x_sent(t - 1, XP_HERE), x_sent(t, XP_HERE))
        send(xm_copy, x_sent(t - 1, XM_HERE), x_sent(t, XM_HERE))
        send(y_copy, y_sent(t - 1), y_sent(t))
        lax.fori_loop(clip(z_count(t - 1), QZ - 1), clip(z_count(t), QZ - 1), zstep, 0)

        @pl.when(t == 0)
        def _():
            remote(theirs, theirs, cs.at[0], orr.at[0], sibling).wait_recv()

        @pl.when((t >= 1) & (t <= QX))
        def _():
            sib_copy(0, t - 1, 1 - c).wait_recv()
            sib_copy(1, t - 1, 1 - c).wait_recv()

        @pl.when((p >= 1) & (p <= QY))
        def _():
            sib_copy(2, p - 1, 1 - c).wait_recv()

        def fresh(i):
            q = jnp.where(i == 2, p - 1, t - 1)
            full = where([(i == 0, group(q, XP_GROUPS)), (i == 1, group(q, XM_GROUPS))], group(q, Y_GROUPS))

            def due():
                j0, t0 = place(0, q)
                j1, t1 = place(1, q)
                j2, t2 = place(2, q)
                j = where([(i == 0, j0), (i == 1, j1)], j2)
                n = jnp.minimum(clip(t - a_slot(j) + 1, 5), full)
                rising = (q < 3) | ((q >= 6) & (q < 11)) | (q == 13) | (q == 14)
                lo = where([(i == 0, t0 - n + 1), (i == 1, t1)], jnp.where(rising, t2 - n + 1, t2))
                return j, lo, n, jnp.int32(0)

            return lax.cond(full > 0, due, lambda: (jnp.int32(0),) * 4)

        event = where([(t < A_SLOTS[0], OWN_SLOT), (t < A_SLOTS[1], A_SLOTS[0]), (t < A_SLOTS[2], A_SLOTS[1])], A_SLOTS[2])
        dist = where([(t < A_SLOTS[0], 0), (t < A_SLOTS[1], 1), (t < A_SLOTS[2], 2)], 3)
        busy = where([(dist == 0, t == event), (dist == 1, (t == event) | (t == event + 2)), (dist == 2, (t == event + 2) | (t == event + 3))], (t == event) | (t == event + 1))

        def waited(i):
            j = lax.rem(z + jnp.where((t == event) | ((dist == 2) & (t == event + 2)), dist, 8 - dist), 8)
            whole = all_came(j) < event

            def part():
                lo = 3 * (i - 3)
                b0, b1, b2 = [jnp.where(came(j, lo + m) < event, 1, 0) for m in range(3)]
                n = b0 + b1 + b2
                gap = jnp.where((n == 2) & (b1 == 0), 1, 0)
                return j, lo + jnp.where(b0 == 1, 0, jnp.where(b1 == 1, 1, 2)), n, gap

            return lax.cond(whole, lambda: (j, jnp.int32(0), jnp.where(i == 3, NT, 0), jnp.int32(0)), part)

        def work(i, _):
            j, lo, n, gap = lax.cond(i < 3, fresh, waited, i)
            for size in (2, 3, 4, 5, NT):

                @pl.when((n == size) & (gap == 0))
                def _(size=size):
                    add(j, lo if size < NT else 0, size)

            def one(m, _):
                add(j, lo + 2 * m, 1)
                return 0

            lax.fori_loop(0, where([(n == 1, 1), (gap == 1, 2)], 0), one, 0)
            return 0

        lax.fori_loop(0, jnp.where(busy, 6, 3), work, 0)
        return 0

    lax.fori_loop(0, SLOTS, slot, 0)

    z_arrival(jnp.int32(QZ - 1), 0).wait_recv()
    z_arrival(jnp.int32(QZ - 1), 1).wait_recv()

    def left_all(ref, sem, to):
        remote(ref, ref, sem, orr.at[0], to).wait_send()

    x_bytes = vbuf.at[pl.ds(0, 4), pl.ds(0, QX * TILE // 4)]
    left_all(x_bytes, xs.at[0], right)
    left_all(x_bytes, xs.at[1], left)
    left_all(vbuf.at[pl.ds(0, 2), pl.ds(0, QY * TILE // 2)], ys.at[0], across)
    left_all(abuf.at[pl.ds(0, QZ * ACH // ROWS)], zs.at[0], up)
    left_all(abuf.at[pl.ds(0, QZ * ACH // ROWS)], zs.at[1], down)
    left_all(abuf.at[0], ps.at[0], pair)
    left_all(vbuf.at[pl.ds(0, ((2 * QX + QY) * TILE + COLS) // COLS)], cs.at[0], sibling)


def finish(vbuf, abuf, acc, o_ref, out, sem):
    z, cd = lax.axis_index("ab") // 2, lax.axis_index("cd")
    far_a = lax.rem(z + 4, 8)
    far_v = (1 - cd // 4) * 4 + lax.rem(cd + 2, 4)
    copies = []
    for g, (lo, hi) in enumerate(CUTS):
        cols = pl.ds(lo * TILE, (hi - lo) * TILE)
        copies.append(pltpu.make_async_copy(out.at[:, cols], o_ref.at[:, cols], sem.at[g]))

    def run(blocks):
        planes = [2 * j + i for j in blocks for i in range(2)]
        a = jnp.concatenate([abuf[k] for k in planes], axis=1)
        for (lo, hi), copy in zip(CUTS, copies):
            rows = pl.ds(lo * TILE, (hi - lo) * TILE)
            b = jnp.concatenate([vbuf[k, rows] for k in planes], axis=1)
            part = lax.dot_general(a, b, (((1,), (1,)), ((), ())), preferred_element_type=jnp.float32)
            for tile in range(lo, hi):
                cols = slice((tile - lo) * TILE, (tile - lo + 1) * TILE)
                out[:, tile * TILE : (tile + 1) * TILE] = (acc[tile] + part[:, cols]).astype(out.dtype)
            copy.start()

    @pl.when(far_a == far_v)
    def _():
        run([far_a])

    @pl.when(far_a != far_v)
    def _():
        run([far_a, far_v])

    for copy in copies:
        copy.wait()


def on_device(integrals, amplitudes):
    dma = pltpu.SemaphoreType.DMA
    args = [pltpu.with_memory_space_constraint(v, pltpu.HBM) for v in (integrals, amplitudes)]
    held = pl.pallas_call(
        kernel,
        out_shape=[
            pltpu.VMEM((16, COLS, BLK), jnp.bfloat16),
            pltpu.VMEM((16, ROWS, BLK), jnp.bfloat16),
            pltpu.VMEM((NT, ROWS, TILE), jnp.float32),
        ],
        in_specs=[pl.BlockSpec(memory_space=pltpu.HBM)] * 2,
        out_specs=[pl.BlockSpec(memory_space=pltpu.VMEM)] * 3,
        scratch_shapes=[
            dma((2,)),
            dma((2,)), dma((2, XSEM)),
            dma((1,)), dma((QY,)),
            dma((1,)), dma((3,)),
            dma((2,)), dma((2, ZSEM)),
            dma((1,)), dma((3, CSEM)),
            dma((1,)),
        ],
        compiler_params=pltpu.CompilerParams(
            collective_id=0, has_side_effects=True, vmem_limit_bytes=24 << 20
        ),
        cost_estimate=pl.CostEstimate(
            flops=2 * ROWS * COLS * 1536, bytes_accessed=1 << 20, transcendentals=0
        ),
        name="ladder",
    )(*args)
    held = [pltpu.with_memory_space_constraint(v, pltpu.VMEM) for v in held]
    return pl.pallas_call(
        finish,
        out_shape=jax.ShapeDtypeStruct((ROWS, COLS), jnp.bfloat16),
        in_specs=[pl.BlockSpec(memory_space=pltpu.VMEM)] * 3,
        out_specs=pl.BlockSpec(memory_space=pltpu.HBM),
        scratch_shapes=[pltpu.VMEM((ROWS, COLS), jnp.bfloat16), dma((len(CUTS),))],
        compiler_params=pltpu.CompilerParams(vmem_limit_bytes=24 << 20),
        cost_estimate=pl.CostEstimate(
            flops=2 * ROWS * COLS * 512, bytes_accessed=4 << 20, transcendentals=0
        ),
        name="finish",
    )(*held)


def solution(mesh):
    in_specs = (P("ab", ("cd", "rep")), P(("cd", "rep"), "ab"))
    out_specs = P(("cd", "rep"), "ab")
    return jax.shard_map(on_device, mesh=mesh, in_specs=in_specs, out_specs=out_specs, check_vma=False)
```

```python
import jax
import jax.numpy as jnp
from jax import lax
from jax.experimental import pallas as pl
from jax.experimental.pallas import tpu as pltpu
from jax.sharding import PartitionSpec as P

MESH = pl.DeviceIdType.MESH
ROWS = 864
COLS = 2304
BLK = 128
TILE = 256
NT = COLS // TILE
ACH = 288
QX, QY, QZ = 23, 17, 21
AHEAD = 6
YAHEAD = 4
ZAHEAD = 3
XSEM, ZSEM, CSEM = 2 * AHEAD, 2 * ZAHEAD, 4
YLAG = 4
SLOTS = QX + 1
CUTS = ((0, 3), (3, 7), (7, 9))


def z_count(t):
    return ((t + 1) * 25) // 28


OWN_SLOT, *A_SLOTS = [next(t for t in range(99) if z_count(t) >= n) for n in (3, 6, 12, 18)]
OWN_TILES = (3, 4, 5, 2, 1, 0, 6, 7, 8)
ZP_HERE = [-1, -1, -1] + list(range(15)) + [12, 13, 15]
ZM_HERE = [-1, -1, -1] + list(range(15)) + [14, 16, 17]
XP_HERE = [0] * 9 + [0, 1, 2, 3, 4] + [YLAG + p for p in (1, 2, 6, 7, 8, 9, 10, 13, 14)]
XM_HERE = [0] * 9 + [0, 1, 2, 3] + [YLAG + p for p in (1, 0, 3, 4, 5)] + [13] + [YLAG + p for p in (11, 12, 15, 16)]

XP_GROUPS = {2: 3, 5: 3, 8: 3, 13: 5, 18: 5, 21: 3}
XM_GROUPS = {3: 4, 8: 5, 12: 4, 17: 5}
Y_GROUPS = {2: 3, 5: 3, 8: 3, 10: 2, 12: 2, 14: 2, 16: 2}


def kernel(v_ref, r_ref, vbuf, abuf, acc, lsem, xs, xr, ys, yr, ps, pr, zs, zr, cs, cr, orr):
    ab, cd, c = lax.axis_index("ab"), lax.axis_index("cd"), lax.axis_index("rep")
    z, yl = ab // 2, lax.rem(ab, 2)
    h, x = cd // 4, lax.rem(cd, 4)

    right, left = (ab, h * 4 + lax.rem(x + 1, 4), c), (ab, h * 4 + lax.rem(x + 3, 4), c)
    across = (ab, (1 - h) * 4 + x, c)
    pair = (z * 2 + 1 - yl, cd, c)
    up, down = (lax.rem(z + 1, 8) * 2 + yl, cd, c), (lax.rem(z + 7, 8) * 2 + yl, cd, c)
    sibling = (ab, cd, 1 - c)

    def remote(src, dst, s, r, to):
        return pltpu.make_async_remote_copy(
            src_ref=src, dst_ref=dst, send_sem=s, recv_sem=r, device_id=to, device_id_type=MESH
        )

    def where(conds, last):
        out = last
        for cond, value in reversed(conds):
            out = jnp.where(cond, value, out)
        return out

    def block(dx, dh):
        hh = h + dh - 2 * h * dh
        return hh * 4 + lax.rem(x + dx, 4)

    def tile_at(j, core, tile):
        return vbuf.at[2 * j + core, pl.ds(pl.multiple_of(tile * TILE, TILE), TILE)]

    def xp(q):
        dx = where([(q < 9, 0), (q < 14, 3), (q < 19, 0)], 3)
        dh = jnp.where(q < 14, 0, 1)
        return dx, dh, q - where([(q < 9, 0), (q < 14, 9), (q < 19, 10)], 19)

    def xm(q):
        dx = where([(q < 9, 0), (q < 13, 1), (q < 18, 0)], 1)
        dh = jnp.where(q < 13, 0, 1)
        return dx, dh, where([(q < 9, 8 - q), (q < 18, 17 - q), (q == 18, 4)], 27 - q)

    def yx(p):
        k = jnp.maximum(p - 9, 0)
        up_half = lax.rem(k // 2, 2) == 0
        i = (k // 4) * 2 + lax.rem(k, 2)
        dx = where([(p < 9, 0), (up_half, 3)], 1)
        return dx, 0, where([(p < 3, p + 3), (p < 6, 5 - p), (p < 9, p), (up_half, i)], 8 - i)

    def xp_copy(q):
        dx, dh, tile = xp(q)
        t = tile_at(block(dx, dh), c, tile)
        return remote(t, t, xs.at[0], xr.at[0, lax.rem(q, XSEM)], right)

    def xm_copy(q):
        dx, dh, tile = xm(q)
        t = tile_at(block(dx, dh), c, tile)
        return remote(t, t, xs.at[1], xr.at[1, lax.rem(q, XSEM)], left)

    def y_copy(p):
        dx, _, tile = yx(p)
        t = tile_at(block(dx, 0), c, tile)
        return remote(t, t, ys.at[0], yr.at[p], across)

    def a_at(zz, y, chunk):
        return abuf.at[2 * zz + y, pl.ds(pl.multiple_of(chunk * ACH, 16), ACH)]

    def z_copy(s, way):
        k = s - 18
        if way == 0:
            tail = where([(k == 0, 18), (k == 1, 19)], 21)
        else:
            tail = where([(k == 0, 20), (k == 1, 22)], 23)
        rr = jnp.where(s < 18, s, tail)
        back, part, chunk = rr // 6, lax.rem(rr, 6) // 3, lax.rem(rr, 3)
        zz = lax.rem(z + (8 - back if way == 0 else back), 8)
        t = a_at(zz, jnp.where(part == 1, 1 - yl, yl), chunk)
        return remote(t, t, zs.at[way], zr.at[way, lax.rem(s, ZSEM)], up if way == 0 else down)

    def place(stream, q):
        if stream == 0:
            dx, dh, tile = xp(q)
            return block(dx + 3, dh), tile
        if stream == 1:
            dx, dh, tile = xm(q)
            return block(dx + 1, dh), tile
        dx, _, tile = yx(q)
        return block(dx, 1), tile

    def sib_copy(stream, q):
        j, tile = place(stream, q)
        t = tile_at(j, c, tile)
        return remote(t, t, cs.at[0], cr.at[stream, lax.rem(q, CSEM)], sibling)

    def got(sem, ref):
        remote(ref, ref, cs.at[0], sem, sibling).wait_recv()

    v_chunk, a_chunk = vbuf.at[0, pl.ds(0, TILE)], abuf.at[0, pl.ds(0, ACH)]

    def pair_copy(i, y):
        t = a_at(z, y, i)
        return remote(t, t, ps.at[0], pr.at[i], pair)

    own_v = pltpu.make_async_copy(v_ref, vbuf.at[2 * cd + c], lsem.at[0])
    own_a = pltpu.make_async_copy(r_ref, abuf.at[2 * z + yl], lsem.at[1])
    own_a.start()
    own_v.start()

    barrier = pltpu.get_barrier_semaphore()
    for other in (right, left, across, pair, up, down, sibling):
        pl.semaphore_signal(barrier, inc=1, device_id=other, device_id_type=MESH)
    pl.semaphore_wait(barrier, 7)

    for i in range(3):
        rows = r_ref.at[pl.ds(i * ACH, ACH)]
        t = a_at(z, yl, i)
        remote(rows, t, ps.at[0], pr.at[i], pair).start()
        remote(rows, t, zs.at[0], zr.at[0, i], up).start()
        remote(rows, t, zs.at[1], zr.at[1, i], down).start()
    mine = vbuf.at[2 * cd + c]
    theirs = vbuf.at[2 * cd + 1 - c]
    for i in range(AHEAD):
        for tile, sem, to in ((i, 0, right), (8 - i, 1, left)):
            rows = v_ref.at[pl.ds(tile * TILE, TILE)]
            remote(rows, tile_at(cd, c, tile), xs.at[sem], xr.at[sem, i], to).start()
        if i < YAHEAD:
            tile = OWN_TILES[i]
            rows = v_ref.at[pl.ds(tile * TILE, TILE)]
            remote(rows, tile_at(cd, c, tile), ys.at[0], yr.at[i], across).start()
    remote(v_ref, mine, cs.at[0], orr.at[0], sibling).start()
    acc[...] = jnp.zeros_like(acc)
    own_a.wait()
    own_v.wait()

    def product(a, j, tile, n):
        rows = pl.ds(pl.multiple_of(tile * TILE, TILE), n * TILE)
        b = jnp.concatenate([vbuf[2 * j, rows], vbuf[2 * j + 1, rows]], axis=1)
        return lax.dot_general(a, b, (((1,), (1,)), ((), ())), preferred_element_type=jnp.float32)

    def add(j, tile, n):
        part = product(jnp.concatenate([abuf[2 * j], abuf[2 * j + 1]], axis=1), j, tile, n)
        for k in range(n):
            acc[tile + k] += part[:, k * TILE : (k + 1) * TILE]

    def clip(v, top):
        return jnp.minimum(jnp.maximum(v, 0), top)

    def a_slot(j):
        d = lax.rem(j - z + 8, 8)
        d = jnp.minimum(d, 8 - d)
        return where([(d == 0, OWN_SLOT), (d == 1, A_SLOTS[0]), (d == 2, A_SLOTS[1]), (d == 3, A_SLOTS[2])], SLOTS)

    def came(j, tile):
        jh, jx = j // 4, lax.rem(j, 4)
        dx = lax.rem(jx - x + 4, 4)
        low = tile < 4
        pos = where([(tile < 3, 5 - tile), (tile < 6, tile - 3)], tile)
        rise = where([(tile < 2, 9 + tile)], 11 + tile) + YLAG + 1
        fall = where([(tile > 6, 19 - tile)], 21 - tile) + YLAG + 1
        near = where([(dx == 0, 0), (dx == 1, 9 - tile), (dx == 3, tile + 1), (tile < 5, tile + 10)], 18 - tile)
        far = where(
            [(dx == 0, pos + YLAG + 1), (dx == 1, jnp.where(tile < 5, 18 - tile, fall)),
             (dx == 3, jnp.where(low, rise, tile + 11)), (tile < 3, tile + 20)],
            99)
        return jnp.where(jh == h, near, far)

    def all_came(j):
        dx = lax.rem(lax.rem(j, 4) - x + 4, 4)
        near = where([(dx == 0, 0), (dx == 2, 14)], 9)
        far = where([(dx == 0, YLAG + 9), (dx == 3, 19), (dx == 1, YLAG + 17)], QX)
        return jnp.where(j // 4 == h, near, far)

    def x_sent(t, here):
        out = jnp.minimum(t + 1 + AHEAD, QX)
        for q, slot in enumerate(here):
            if slot > q - AHEAD:
                out = jnp.minimum(out, jnp.where(t >= slot, QX, q)) if q >= AHEAD else out
        return out

    def y_sent(t):
        return jnp.minimum(t + 1 + YAHEAD, QY)

    def group(q, groups):
        return where([(q == last, n) for last, n in groups.items()], 0)

    def send(copy, lo, hi):
        def one(q, _):
            copy(q).start()
            return 0

        lax.fori_loop(lo, hi, one, 0)

    def z_sent(r, here):
        out = jnp.minimum(r + 1 + ZAHEAD, QZ)
        for q, step in enumerate(here):
            if step > q - ZAHEAD:
                out = jnp.minimum(out, jnp.where(r >= step, QZ, q))
        return out

    def zstep(r, _):
        got(zr.at[0, lax.rem(r, ZSEM)], a_chunk)
        got(zr.at[1, lax.rem(r, ZSEM)], a_chunk)

        @pl.when(r < 3)
        def _():
            got(pr.at[r], a_chunk)

        send(lambda q: z_copy(q, 0), z_sent(r - 1, ZP_HERE), z_sent(r, ZP_HERE))
        send(lambda q: z_copy(q, 1), z_sent(r - 1, ZM_HERE), z_sent(r, ZM_HERE))
        return 0

    def slot(t, _):
        p = t - YLAG

        @pl.when(t < QX)
        def _():
            got(xr.at[0, lax.rem(t, XSEM)], v_chunk)
            sib_copy(0, t).start()
            got(xr.at[1, lax.rem(t, XSEM)], v_chunk)
            sib_copy(1, t).start()

        @pl.when((p >= 0) & (p < QY))
        def _():
            got(yr.at[p], v_chunk)
            sib_copy(2, p).start()

        send(xp_copy, x_sent(t - 1, XP_HERE), x_sent(t, XP_HERE))
        send(xm_copy, x_sent(t - 1, XM_HERE), x_sent(t, XM_HERE))
        send(y_copy, y_sent(t - 1), y_sent(t))
        lax.fori_loop(clip(z_count(t - 1), QZ - 1), clip(z_count(t), QZ - 1), zstep, 0)

        @pl.when(t == 0)
        def _():
            remote(theirs, theirs, cs.at[0], orr.at[0], sibling).wait_recv()

        @pl.when((t >= 1) & (t <= QX))
        def _():
            got(cr.at[0, lax.rem(t - 1, CSEM)], v_chunk)
            got(cr.at[1, lax.rem(t - 1, CSEM)], v_chunk)

        @pl.when((p >= 1) & (p <= QY))
        def _():
            got(cr.at[2, lax.rem(p - 1, CSEM)], v_chunk)

        def fresh(i):
            q = jnp.where(i == 2, p - 1, t - 1)
            full = where([(i == 0, group(q, XP_GROUPS)), (i == 1, group(q, XM_GROUPS))], group(q, Y_GROUPS))

            def due():
                j0, t0 = place(0, q)
                j1, t1 = place(1, q)
                j2, t2 = place(2, q)
                j = where([(i == 0, j0), (i == 1, j1)], j2)
                n = jnp.minimum(clip(t - a_slot(j) + 1, 5), full)
                rising = (q < 3) | ((q >= 6) & (q < 11)) | (q == 13) | (q == 14)
                lo = where([(i == 0, t0 - n + 1), (i == 1, t1)], jnp.where(rising, t2 - n + 1, t2))
                return j, lo, n, jnp.int32(0)

            return lax.cond(full > 0, due, lambda: (jnp.int32(0),) * 4)

        event = where([(t < A_SLOTS[0], OWN_SLOT), (t < A_SLOTS[1], A_SLOTS[0]), (t < A_SLOTS[2], A_SLOTS[1])], A_SLOTS[2])
        dist = where([(t < A_SLOTS[0], 0), (t < A_SLOTS[1], 1), (t < A_SLOTS[2], 2)], 3)
        busy = where([(dist == 0, t == event), (dist == 1, (t == event) | (t == event + 2)), (dist == 2, (t == event + 2) | (t == event + 3))], (t == event) | (t == event + 1))

        def waited(i):
            j = lax.rem(z + jnp.where((t == event) | ((dist == 2) & (t == event + 2)), dist, 8 - dist), 8)
            whole = all_came(j) < event

            def part():
                lo = 3 * (i - 3)
                b0, b1, b2 = [jnp.where(came(j, lo + m) < event, 1, 0) for m in range(3)]
                n = b0 + b1 + b2
                gap = jnp.where((n == 2) & (b1 == 0), 1, 0)
                return j, lo + jnp.where(b0 == 1, 0, jnp.where(b1 == 1, 1, 2)), n, gap

            return lax.cond(whole, lambda: (j, jnp.int32(0), jnp.where(i == 3, NT, 0), jnp.int32(0)), part)

        def work(i, _):
            j, lo, n, gap = lax.cond(i < 3, fresh, waited, i)
            for size in (2, 3, 4, 5, NT):

                @pl.when((n == size) & (gap == 0))
                def _(size=size):
                    add(j, lo if size < NT else 0, size)

            def one(m, _):
                add(j, lo + 2 * m, 1)
                return 0

            lax.fori_loop(0, where([(n == 1, 1), (gap == 1, 2)], 0), one, 0)
            return 0

        lax.fori_loop(0, jnp.where(busy, 6, 3), work, 0)
        return 0

    lax.fori_loop(0, SLOTS, slot, 0)

    got(zr.at[0, (QZ - 1) % ZSEM], a_chunk)
    got(zr.at[1, (QZ - 1) % ZSEM], a_chunk)

    def left_all(ref, sem, to):
        remote(ref, ref, sem, orr.at[0], to).wait_send()

    x_bytes = vbuf.at[pl.ds(0, 4), pl.ds(0, QX * TILE // 4)]
    left_all(x_bytes, xs.at[0], right)
    left_all(x_bytes, xs.at[1], left)
    left_all(vbuf.at[pl.ds(0, 2), pl.ds(0, QY * TILE // 2)], ys.at[0], across)
    left_all(abuf.at[pl.ds(0, QZ * ACH // ROWS)], zs.at[0], up)
    left_all(abuf.at[pl.ds(0, QZ * ACH // ROWS)], zs.at[1], down)
    left_all(abuf.at[0], ps.at[0], pair)
    left_all(vbuf.at[pl.ds(0, ((2 * QX + QY) * TILE + COLS) // COLS)], cs.at[0], sibling)


def finish(vbuf, abuf, acc, o_ref, out, sem):
    z, cd = lax.axis_index("ab") // 2, lax.axis_index("cd")
    far_a = lax.rem(z + 4, 8)
    far_v = (1 - cd // 4) * 4 + lax.rem(cd + 2, 4)
    copies = []
    for g, (lo, hi) in enumerate(CUTS):
        cols = pl.ds(lo * TILE, (hi - lo) * TILE)
        copies.append(pltpu.make_async_copy(out.at[:, cols], o_ref.at[:, cols], sem.at[g]))

    def part(g, blocks):
        planes = [2 * j + i for j in blocks for i in range(2)]
        lo, hi = CUTS[g]
        rows = pl.ds(lo * TILE, (hi - lo) * TILE)
        a = jnp.concatenate([abuf[k] for k in planes], axis=1)
        b = jnp.concatenate([vbuf[k, rows] for k in planes], axis=1)
        summed = lax.dot_general(a, b, (((1,), (1,)), ((), ())), preferred_element_type=jnp.float32)
        for tile in range(lo, hi):
            cols = slice((tile - lo) * TILE, (tile - lo + 1) * TILE)
            out[:, tile * TILE : (tile + 1) * TILE] = (acc[tile] + summed[:, cols]).astype(out.dtype)
        copies[g].start()

    part(0, [far_a])

    @pl.when(far_a == far_v)
    def _():
        for g in range(1, len(CUTS)):
            part(g, [far_a])

    @pl.when(far_a != far_v)
    def _():
        for g in range(1, len(CUTS)):
            part(g, [far_a, far_v])

    for copy in copies:
        copy.wait()


def on_device(integrals, amplitudes):
    dma = pltpu.SemaphoreType.DMA
    args = [pltpu.with_memory_space_constraint(v, pltpu.HBM) for v in (integrals, amplitudes)]
    held = pl.pallas_call(
        kernel,
        out_shape=[
            pltpu.VMEM((16, COLS, BLK), jnp.bfloat16),
            pltpu.VMEM((16, ROWS, BLK), jnp.bfloat16),
            pltpu.VMEM((NT, ROWS, TILE), jnp.float32),
        ],
        in_specs=[pl.BlockSpec(memory_space=pltpu.HBM)] * 2,
        out_specs=[pl.BlockSpec(memory_space=pltpu.VMEM)] * 3,
        scratch_shapes=[
            dma((2,)),
            dma((2,)), dma((2, XSEM)),
            dma((1,)), dma((QY,)),
            dma((1,)), dma((3,)),
            dma((2,)), dma((2, ZSEM)),
            dma((1,)), dma((3, CSEM)),
            dma((1,)),
        ],
        compiler_params=pltpu.CompilerParams(
            collective_id=0, has_side_effects=True, vmem_limit_bytes=24 << 20
        ),
        cost_estimate=pl.CostEstimate(
            flops=2 * ROWS * COLS * 1536, bytes_accessed=1 << 20, transcendentals=0
        ),
        name="ladder",
    )(*args)
    held = [pltpu.with_memory_space_constraint(v, pltpu.VMEM) for v in held]
    return pl.pallas_call(
        finish,
        out_shape=jax.ShapeDtypeStruct((ROWS, COLS), jnp.bfloat16),
        in_specs=[pl.BlockSpec(memory_space=pltpu.VMEM)] * 3,
        out_specs=pl.BlockSpec(memory_space=pltpu.HBM),
        scratch_shapes=[pltpu.VMEM((ROWS, COLS), jnp.bfloat16), dma((len(CUTS),))],
        compiler_params=pltpu.CompilerParams(vmem_limit_bytes=24 << 20),
        cost_estimate=pl.CostEstimate(
            flops=2 * ROWS * COLS * 512, bytes_accessed=4 << 20, transcendentals=0
        ),
        name="finish",
    )(*held)


def solution(mesh):
    in_specs = (P("ab", ("cd", "rep")), P(("cd", "rep"), "ab"))
    out_specs = P(("cd", "rep"), "ab")
    return jax.shard_map(on_device, mesh=mesh, in_specs=in_specs, out_specs=out_specs, check_vma=False)
```

```python
import jax
import jax.numpy as jnp
from jax import lax
from jax.experimental import pallas as pl
from jax.experimental.pallas import tpu as pltpu
from jax.sharding import PartitionSpec as P

MESH = pl.DeviceIdType.MESH
ROWS = 864
COLS = 2304
BLK = 128
TILE = 256
NT = COLS // TILE
ACH = 288
QX, QY, QZ = 23, 17, 21
AHEAD = 6
YAHEAD = 4
ZAHEAD = 3
XSEM, ZSEM, CSEM = 2 * AHEAD, 2 * ZAHEAD, 4
YLAG = 4
SLOTS = QX + 1
CUTS = ((0, 3), (3, 7), (7, 9))


def z_count(t):
    return ((t + 1) * 25) // 28


OWN_SLOT, *A_SLOTS = [next(t for t in range(99) if z_count(t) >= n) for n in (3, 6, 12, 18)]
OWN_TILES = (3, 4, 5, 2, 1, 0, 6, 7, 8)
ZP_HERE = [-1, -1, -1] + list(range(15)) + [12, 13, 15]
ZM_HERE = [-1, -1, -1] + list(range(15)) + [14, 16, 17]
XP_HERE = [0] * 9 + [0, 1, 2, 3, 4] + [YLAG + p for p in (1, 2, 6, 7, 8, 9, 10, 13, 14)]
XM_HERE = [0] * 9 + [0, 1, 2, 3] + [YLAG + p for p in (1, 0, 3, 4, 5)] + [13] + [YLAG + p for p in (11, 12, 15, 16)]

XP_GROUPS = {2: 3, 5: 3, 8: 3, 13: 5, 18: 5, 21: 3}
XM_GROUPS = {3: 4, 8: 5, 12: 4, 17: 5}
Y_GROUPS = {2: 3, 5: 3, 8: 3, 10: 2, 12: 2, 14: 2, 16: 2}


def kernel(v_ref, r_ref, vbuf, abuf, acc, lsem, xs, xr, ys, yr, ps, pr, zs, zr, cs, cr, orr):
    ab, cd, c = lax.axis_index("ab"), lax.axis_index("cd"), lax.axis_index("rep")
    z, yl = ab // 2, lax.rem(ab, 2)
    h, x = cd // 4, lax.rem(cd, 4)

    right, left = (ab, h * 4 + lax.rem(x + 1, 4), c), (ab, h * 4 + lax.rem(x + 3, 4), c)
    across = (ab, (1 - h) * 4 + x, c)
    pair = (z * 2 + 1 - yl, cd, c)
    up, down = (lax.rem(z + 1, 8) * 2 + yl, cd, c), (lax.rem(z + 7, 8) * 2 + yl, cd, c)
    sibling = (ab, cd, 1 - c)

    def remote(src, dst, s, r, to):
        return pltpu.make_async_remote_copy(
            src_ref=src, dst_ref=dst, send_sem=s, recv_sem=r, device_id=to, device_id_type=MESH
        )

    def where(conds, last):
        out = last
        for cond, value in reversed(conds):
            out = jnp.where(cond, value, out)
        return out

    def block(dx, dh):
        hh = h + dh - 2 * h * dh
        return hh * 4 + lax.rem(x + dx, 4)

    def tile_at(j, core, tile):
        return vbuf.at[2 * j + core, pl.ds(pl.multiple_of(tile * TILE, TILE), TILE)]

    def xp(q):
        dx = where([(q < 9, 0), (q < 14, 3), (q < 19, 0)], 3)
        dh = jnp.where(q < 14, 0, 1)
        return dx, dh, q - where([(q < 9, 0), (q < 14, 9), (q < 19, 10)], 19)

    def xm(q):
        dx = where([(q < 9, 0), (q < 13, 1), (q < 18, 0)], 1)
        dh = jnp.where(q < 13, 0, 1)
        return dx, dh, where([(q < 9, 8 - q), (q < 18, 17 - q), (q == 18, 4)], 27 - q)

    def yx(p):
        k = jnp.maximum(p - 9, 0)
        up_half = lax.rem(k // 2, 2) == 0
        i = (k // 4) * 2 + lax.rem(k, 2)
        dx = where([(p < 9, 0), (up_half, 3)], 1)
        return dx, 0, where([(p < 3, p + 3), (p < 6, 5 - p), (p < 9, p), (up_half, i)], 8 - i)

    def xp_copy(q):
        dx, dh, tile = xp(q)
        t = tile_at(block(dx, dh), c, tile)
        return remote(t, t, xs.at[0], xr.at[0, lax.rem(q, XSEM)], right)

    def xm_copy(q):
        dx, dh, tile = xm(q)
        t = tile_at(block(dx, dh), c, tile)
        return remote(t, t, xs.at[1], xr.at[1, lax.rem(q, XSEM)], left)

    def y_copy(p):
        dx, _, tile = yx(p)
        t = tile_at(block(dx, 0), c, tile)
        return remote(t, t, ys.at[0], yr.at[p], across)

    def a_at(zz, y, chunk):
        return abuf.at[2 * zz + y, pl.ds(pl.multiple_of(chunk * ACH, 16), ACH)]

    def z_copy(s, way):
        k = s - 18
        if way == 0:
            tail = where([(k == 0, 18), (k == 1, 19)], 21)
        else:
            tail = where([(k == 0, 20), (k == 1, 22)], 23)
        rr = jnp.where(s < 18, s, tail)
        back, part, chunk = rr // 6, lax.rem(rr, 6) // 3, lax.rem(rr, 3)
        zz = lax.rem(z + (8 - back if way == 0 else back), 8)
        t = a_at(zz, jnp.where(part == 1, 1 - yl, yl), chunk)
        return remote(t, t, zs.at[way], zr.at[way, lax.rem(s, ZSEM)], up if way == 0 else down)

    def place(stream, q):
        if stream == 0:
            dx, dh, tile = xp(q)
            return block(dx + 3, dh), tile
        if stream == 1:
            dx, dh, tile = xm(q)
            return block(dx + 1, dh), tile
        dx, _, tile = yx(q)
        return block(dx, 1), tile

    def sib_copy(stream, q):
        j, tile = place(stream, q)
        t = tile_at(j, c, tile)
        return remote(t, t, cs.at[0], cr.at[stream, lax.rem(q, CSEM)], sibling)

    def got(sem, ref):
        remote(ref, ref, cs.at[0], sem, sibling).wait_recv()

    v_chunk, a_chunk = vbuf.at[0, pl.ds(0, TILE)], abuf.at[0, pl.ds(0, ACH)]

    def pair_copy(i, y):
        t = a_at(z, y, i)
        return remote(t, t, ps.at[0], pr.at[i], pair)

    own_v = pltpu.make_async_copy(v_ref, vbuf.at[2 * cd + c], lsem.at[0])
    own_a = pltpu.make_async_copy(r_ref, abuf.at[2 * z + yl], lsem.at[1])
    own_a.start()
    own_v.start()

    barrier = pltpu.get_barrier_semaphore()
    for other in (right, left, across, pair, up, down, sibling):
        pl.semaphore_signal(barrier, inc=1, device_id=other, device_id_type=MESH)
    pl.semaphore_wait(barrier, 7)

    for i in range(3):
        rows = r_ref.at[pl.ds(i * ACH, ACH)]
        t = a_at(z, yl, i)
        remote(rows, t, ps.at[0], pr.at[i], pair).start()
        remote(rows, t, zs.at[0], zr.at[0, i], up).start()
        remote(rows, t, zs.at[1], zr.at[1, i], down).start()
    mine = vbuf.at[2 * cd + c]
    theirs = vbuf.at[2 * cd + 1 - c]
    for i in range(AHEAD):
        for tile, sem, to in ((i, 0, right), (8 - i, 1, left)):
            rows = v_ref.at[pl.ds(tile * TILE, TILE)]
            remote(rows, tile_at(cd, c, tile), xs.at[sem], xr.at[sem, i], to).start()
        if i < YAHEAD:
            tile = OWN_TILES[i]
            rows = v_ref.at[pl.ds(tile * TILE, TILE)]
            remote(rows, tile_at(cd, c, tile), ys.at[0], yr.at[i], across).start()
    remote(v_ref, mine, cs.at[0], orr.at[0], sibling).start()
    acc[...] = jnp.zeros_like(acc)
    own_a.wait()
    own_v.wait()

    def product(a, j, tile, n):
        rows = pl.ds(pl.multiple_of(tile * TILE, TILE), n * TILE)
        b = jnp.concatenate([vbuf[2 * j, rows], vbuf[2 * j + 1, rows]], axis=1)
        return lax.dot_general(a, b, (((1,), (1,)), ((), ())), preferred_element_type=jnp.float32)

    def add(j, tile, n):
        part = product(jnp.concatenate([abuf[2 * j], abuf[2 * j + 1]], axis=1), j, tile, n)
        for k in range(n):
            acc[tile + k] += part[:, k * TILE : (k + 1) * TILE]

    def clip(v, top):
        return jnp.minimum(jnp.maximum(v, 0), top)

    def a_slot(j):
        d = lax.rem(j - z + 8, 8)
        d = where([(d < 5, d), (d == 5, 4)], 8 - d)
        return where([(d == 0, OWN_SLOT), (d == 1, A_SLOTS[0]), (d == 2, A_SLOTS[1]), (d == 3, A_SLOTS[2])], SLOTS)

    def came(j, tile):
        jh, jx = j // 4, lax.rem(j, 4)
        dx = lax.rem(jx - x + 4, 4)
        low = tile < 4
        pos = where([(tile < 3, 5 - tile), (tile < 6, tile - 3)], tile)
        rise = where([(tile < 2, 9 + tile)], 11 + tile) + YLAG + 1
        fall = where([(tile > 6, 19 - tile)], 21 - tile) + YLAG + 1
        near = where([(dx == 0, 0), (dx == 1, 9 - tile), (dx == 3, tile + 1), (tile < 5, tile + 10)], 18 - tile)
        far = where(
            [(dx == 0, pos + YLAG + 1), (dx == 1, jnp.where(tile < 5, 18 - tile, fall)),
             (dx == 3, jnp.where(low, rise, tile + 11)), (tile < 3, tile + 20)],
            99)
        return jnp.where(jh == h, near, far)

    def all_came(j):
        dx = lax.rem(lax.rem(j, 4) - x + 4, 4)
        near = where([(dx == 0, 0), (dx == 2, 14)], 9)
        far = where([(dx == 0, YLAG + 9), (dx == 3, 19), (dx == 1, YLAG + 17)], QX)
        return jnp.where(j // 4 == h, near, far)

    def x_sent(t, here):
        out = jnp.minimum(t + 1 + AHEAD, QX)
        for q, slot in enumerate(here):
            if slot > q - AHEAD:
                out = jnp.minimum(out, jnp.where(t >= slot, QX, q)) if q >= AHEAD else out
        return out

    def y_sent(t):
        return jnp.minimum(t + 1 + YAHEAD, QY)

    def group(q, groups):
        return where([(q == last, n) for last, n in groups.items()], 0)

    def send(copy, lo, hi):
        def one(q, _):
            copy(q).start()
            return 0

        lax.fori_loop(lo, hi, one, 0)

    def z_sent(r, here):
        out = jnp.minimum(r + 1 + ZAHEAD, QZ)
        for q, step in enumerate(here):
            if step > q - ZAHEAD:
                out = jnp.minimum(out, jnp.where(r >= step, QZ, q))
        return out

    def zstep(r, _):
        got(zr.at[0, lax.rem(r, ZSEM)], a_chunk)
        got(zr.at[1, lax.rem(r, ZSEM)], a_chunk)

        @pl.when(r < 3)
        def _():
            got(pr.at[r], a_chunk)

        send(lambda q: z_copy(q, 0), z_sent(r - 1, ZP_HERE), z_sent(r, ZP_HERE))
        send(lambda q: z_copy(q, 1), z_sent(r - 1, ZM_HERE), z_sent(r, ZM_HERE))
        return 0

    def slot(t, _):
        p = t - YLAG

        @pl.when(t < QX)
        def _():
            got(xr.at[0, lax.rem(t, XSEM)], v_chunk)
            sib_copy(0, t).start()
            got(xr.at[1, lax.rem(t, XSEM)], v_chunk)
            sib_copy(1, t).start()

        @pl.when((p >= 0) & (p < QY))
        def _():
            got(yr.at[p], v_chunk)
            sib_copy(2, p).start()

        send(xp_copy, x_sent(t - 1, XP_HERE), x_sent(t, XP_HERE))
        send(xm_copy, x_sent(t - 1, XM_HERE), x_sent(t, XM_HERE))
        send(y_copy, y_sent(t - 1), y_sent(t))
        lax.fori_loop(clip(z_count(t - 1), QZ - 1), clip(z_count(t), QZ - 1), zstep, 0)

        @pl.when(t == 0)
        def _():
            remote(theirs, theirs, cs.at[0], orr.at[0], sibling).wait_recv()

        @pl.when((t >= 1) & (t <= QX))
        def _():
            got(cr.at[0, lax.rem(t - 1, CSEM)], v_chunk)
            got(cr.at[1, lax.rem(t - 1, CSEM)], v_chunk)

        @pl.when((p >= 1) & (p <= QY))
        def _():
            got(cr.at[2, lax.rem(p - 1, CSEM)], v_chunk)

        def fresh(i):
            q = jnp.where(i == 2, p - 1, t - 1)
            full = where([(i == 0, group(q, XP_GROUPS)), (i == 1, group(q, XM_GROUPS))], group(q, Y_GROUPS))

            def due():
                j0, t0 = place(0, q)
                j1, t1 = place(1, q)
                j2, t2 = place(2, q)
                j = where([(i == 0, j0), (i == 1, j1)], j2)
                n = jnp.minimum(clip(t - a_slot(j) + 1, 5), full)
                rising = (q < 3) | ((q >= 6) & (q < 11)) | (q == 13) | (q == 14)
                lo = where([(i == 0, t0 - n + 1), (i == 1, t1)], jnp.where(rising, t2 - n + 1, t2))
                return j, lo, n, jnp.int32(0)

            return lax.cond(full > 0, due, lambda: (jnp.int32(0),) * 4)

        event = where([(t < A_SLOTS[0], OWN_SLOT), (t < A_SLOTS[1], A_SLOTS[0]), (t < A_SLOTS[2], A_SLOTS[1])], A_SLOTS[2])
        dist = where([(t < A_SLOTS[0], 0), (t < A_SLOTS[1], 1), (t < A_SLOTS[2], 2)], 3)
        busy = where([(dist == 0, t == event), (dist == 1, (t == event) | (t == event + 2)), (dist == 2, (t == event + 2) | (t == event + 3))], t == event)

        def waited(i):
            j = lax.rem(z + jnp.where((t == event) | ((dist == 2) & (t == event + 2)), dist, 8 - dist), 8)
            whole = all_came(j) < event

            def part():
                lo = 3 * (i - 3)
                b0, b1, b2 = [jnp.where(came(j, lo + m) < event, 1, 0) for m in range(3)]
                n = b0 + b1 + b2
                gap = jnp.where((n == 2) & (b1 == 0), 1, 0)
                return j, lo + jnp.where(b0 == 1, 0, jnp.where(b1 == 1, 1, 2)), n, gap

            return lax.cond(whole, lambda: (j, jnp.int32(0), jnp.where(i == 3, NT, 0), jnp.int32(0)), part)

        def work(i, _):
            j, lo, n, gap = lax.cond(i < 3, fresh, waited, i)
            for size in (2, 3, 4, 5, NT):

                @pl.when((n == size) & (gap == 0))
                def _(size=size):
                    add(j, lo if size < NT else 0, size)

            def one(m, _):
                add(j, lo + 2 * m, 1)
                return 0

            lax.fori_loop(0, where([(n == 1, 1), (gap == 1, 2)], 0), one, 0)
            return 0

        lax.fori_loop(0, jnp.where(busy, 6, 3), work, 0)
        return 0

    lax.fori_loop(0, SLOTS, slot, 0)

    got(zr.at[0, (QZ - 1) % ZSEM], a_chunk)
    got(zr.at[1, (QZ - 1) % ZSEM], a_chunk)

    def left_all(ref, sem, to):
        remote(ref, ref, sem, orr.at[0], to).wait_send()

    x_bytes = vbuf.at[pl.ds(0, 4), pl.ds(0, QX * TILE // 4)]
    left_all(x_bytes, xs.at[0], right)
    left_all(x_bytes, xs.at[1], left)
    left_all(vbuf.at[pl.ds(0, 2), pl.ds(0, QY * TILE // 2)], ys.at[0], across)
    left_all(abuf.at[pl.ds(0, QZ * ACH // ROWS)], zs.at[0], up)
    left_all(abuf.at[pl.ds(0, QZ * ACH // ROWS)], zs.at[1], down)
    left_all(abuf.at[0], ps.at[0], pair)
    left_all(vbuf.at[pl.ds(0, ((2 * QX + QY) * TILE + COLS) // COLS)], cs.at[0], sibling)


def finish(vbuf, abuf, acc, o_ref, out, sem):
    z, cd = lax.axis_index("ab") // 2, lax.axis_index("cd")
    far_a = lax.rem(z + 4, 8)
    far_v = (1 - cd // 4) * 4 + lax.rem(cd + 2, 4)
    copies = []
    for g, (lo, hi) in enumerate(CUTS):
        cols = pl.ds(lo * TILE, (hi - lo) * TILE)
        copies.append(pltpu.make_async_copy(out.at[:, cols], o_ref.at[:, cols], sem.at[g]))

    def part(g, blocks):
        planes = [2 * j + i for j in blocks for i in range(2)]
        lo, hi = CUTS[g]
        rows = pl.ds(lo * TILE, (hi - lo) * TILE)
        a = jnp.concatenate([abuf[k] for k in planes], axis=1)
        b = jnp.concatenate([vbuf[k, rows] for k in planes], axis=1)
        summed = lax.dot_general(a, b, (((1,), (1,)), ((), ())), preferred_element_type=jnp.float32)
        for tile in range(lo, hi):
            cols = slice((tile - lo) * TILE, (tile - lo + 1) * TILE)
            out[:, tile * TILE : (tile + 1) * TILE] = (acc[tile] + summed[:, cols]).astype(out.dtype)
        copies[g].start()

    late_a = lax.rem(z + 5, 8)
    both = (far_a == far_v) | (late_a == far_v)
    part(0, [far_a, late_a])

    @pl.when(both)
    def _():
        for g in range(1, len(CUTS)):
            part(g, [far_a, late_a])

    @pl.when(jnp.logical_not(both))
    def _():
        for g in range(1, len(CUTS)):
            part(g, [far_a, late_a, far_v])

    for copy in copies:
        copy.wait()


def on_device(integrals, amplitudes):
    dma = pltpu.SemaphoreType.DMA
    args = [pltpu.with_memory_space_constraint(v, pltpu.HBM) for v in (integrals, amplitudes)]
    held = pl.pallas_call(
        kernel,
        out_shape=[
            pltpu.VMEM((16, COLS, BLK), jnp.bfloat16),
            pltpu.VMEM((16, ROWS, BLK), jnp.bfloat16),
            pltpu.VMEM((NT, ROWS, TILE), jnp.float32),
        ],
        in_specs=[pl.BlockSpec(memory_space=pltpu.HBM)] * 2,
        out_specs=[pl.BlockSpec(memory_space=pltpu.VMEM)] * 3,
        scratch_shapes=[
            dma((2,)),
            dma((2,)), dma((2, XSEM)),
            dma((1,)), dma((QY,)),
            dma((1,)), dma((3,)),
            dma((2,)), dma((2, ZSEM)),
            dma((1,)), dma((3, CSEM)),
            dma((1,)),
        ],
        compiler_params=pltpu.CompilerParams(
            collective_id=0, has_side_effects=True, vmem_limit_bytes=24 << 20
        ),
        cost_estimate=pl.CostEstimate(
            flops=2 * ROWS * COLS * 1536, bytes_accessed=1 << 20, transcendentals=0
        ),
        name="ladder",
    )(*args)
    held = [pltpu.with_memory_space_constraint(v, pltpu.VMEM) for v in held]
    return pl.pallas_call(
        finish,
        out_shape=jax.ShapeDtypeStruct((ROWS, COLS), jnp.bfloat16),
        in_specs=[pl.BlockSpec(memory_space=pltpu.VMEM)] * 3,
        out_specs=pl.BlockSpec(memory_space=pltpu.HBM),
        scratch_shapes=[pltpu.VMEM((ROWS, COLS), jnp.bfloat16), dma((len(CUTS),))],
        compiler_params=pltpu.CompilerParams(vmem_limit_bytes=24 << 20),
        cost_estimate=pl.CostEstimate(
            flops=2 * ROWS * COLS * 512, bytes_accessed=4 << 20, transcendentals=0
        ),
        name="finish",
    )(*held)


def solution(mesh):
    in_specs = (P("ab", ("cd", "rep")), P(("cd", "rep"), "ab"))
    out_specs = P(("cd", "rep"), "ab")
    return jax.shard_map(on_device, mesh=mesh, in_specs=in_specs, out_specs=out_specs, check_vma=False)
```
